32 devices in a mesh: sy: 8 (over y, x, core), sx: 4 (over z).
Axes of the slice: x: 2, y: 2, z: 4, core: 2. Of those that a mesh axis runs over, the one named last changes fastest.
Arguments:
- object_tile: float32 [2, 1024, 512], P(None, 'sy', 'sx'), may hold values from -5 to 5
- probe_modes: float32 [2, 2, 128, 128], replicated, may hold values from -4 to 4
- scan_offsets: int32 [8, 4, 4, 2], P('sy', 'sx'), may hold values from 0 to 128
- intensities: float32 [8, 4, 4, 128, 128], P('sy', 'sx'), may hold values from 0 to 2
Outputs:
- object_out: float32 [2, 1024, 512], P(None, 'sy', 'sx')
- probe_out: float32 [2, 2, 128, 128], replicated
The draws below stay inside these ranges and needn't reach their ends.
Inputs may be any that keep to these rules, and one draw needn't show every extreme that they name: `scan_offsets`: offsets are counted from 64 pixels above and to the left of the device's tile, so a patch stays within 64 pixels of its tile.
All inputs are finite; a program needn't handle non-finite values.
Results may differ from the reference program's by a relative error of at most 0.0003.
Values sent between devices are 32-bit elements; how exact they have to be, the bound alone decides.
No kernel may reach another device: no remote copies, remote signals or barrier semaphores. Data moves between devices by JAX's collectives and lax.ppermute only.
A program may use at most 64 MiB of HBM per device.

```python
import jax
import jax.numpy as jnp
from jax import lax

PATCH = 128
MODES = 2
TILE = 128
NPOS = 4
ITERS = 2
HALF = 64
OBJ_Y = 1024
OBJ_X = 512
N_SY = 8
N_SX = 4


def set_ends(drawn, stream_key, smallest, top_value):
    index_at = [jax.random.randint(jax.random.fold_in(stream_key, axis), (), 0, length) for axis, length in enumerate(drawn.shape)]
    longest = drawn.shape.index(max(drawn.shape))
    next_to = index_at[:longest] + [(index_at[longest] + 1) % drawn.shape[longest]] + index_at[longest + 1:]
    return drawn.at[tuple(index_at)].set(smallest).at[tuple(next_to)].set(top_value)


def level_of(key, dims, cuts, least, top_value):
    def one(axis_at, parts):
        steps = jax.random.uniform(jax.random.fold_in(jax.random.fold_in(key, 6), axis_at), (parts,), jnp.float32, least / len(cuts), top_value / len(cuts))
        return jnp.repeat(jnp.exp(steps), dims[axis_at] // parts).reshape((-1,) + (1,) * (len(dims) - axis_at - 1))

    level = one(*cuts[0])
    for cut in cuts[1:]:
        level = level * one(*cut)
    return level


def centred(own_key, shape, width, most, shards=(), held_as=jnp.bfloat16):
    factor_of = level_of(own_key, shape, shards, -0.22, 0.18) if shards else 1.0
    entries = jax.random.normal(own_key, shape, jnp.float32) * width * factor_of
    return jnp.minimum(jnp.maximum(entries, -most), most).astype(held_as)


def setup_inputs(seed: int = 0) -> dict:
    keys = jax.random.split(jax.random.key(seed), 5)
    object_tile = centred(keys[0], (2, OBJ_Y, OBJ_X), 0.7, 5.0, ((1, 8), (2, 4)), jnp.float32)
    probe_modes = centred(keys[1], (MODES, 2, PATCH, PATCH), 0.5, 4.0, (), jnp.float32)
    scan_offsets = set_ends(jax.random.randint(keys[2], (N_SY, N_SX, NPOS, 2), 0, TILE + 1), jax.random.fold_in(keys[2], 1), 0, TILE).astype(jnp.int32)
    intensities = jnp.clip(2.0 * jax.random.uniform(keys[3], (N_SY, N_SX, NPOS, PATCH, PATCH), jnp.float32) ** level_of(keys[3], (N_SY, N_SX, NPOS, PATCH, PATCH), ((0, 8), (1, 4)), -0.2, 0.2), 0.0, 2.0)
    return dict(object_tile=object_tile, probe_modes=probe_modes, scan_offsets=scan_offsets, intensities=intensities)


OBJECT_STEP = 0.5
PROBE_STEP = 2.0
REGULAR = 1.0


def back_waves(object_real, object_imag, probe_modes, measured):
    probe_cplx = probe_modes[:, 0] + 1j * probe_modes[:, 1]
    patch_cplx = object_real + 1j * object_imag
    exit_wave = probe_cplx[None] * patch_cplx[:, None]
    spectrum = jnp.fft.fft2(exit_wave, norm="ortho")
    power = jnp.real(spectrum) * jnp.real(spectrum) + jnp.imag(spectrum) * jnp.imag(spectrum)
    misfit = jnp.sum(power, axis=1) - measured
    returned = jnp.fft.ifft2(misfit[:, None] * spectrum, norm="ortho")
    return jnp.real(returned), jnp.imag(returned)


def one_pass(canvas, probe_modes, scan_offsets, intensities):
    probe_real = probe_modes[:, 0][None]
    probe_imag = probe_modes[:, 1][None]

    def row_block(carry, inputs):
        gradients, numerator, denominator = carry
        row_number, offsets, measured = inputs
        column_base = (jnp.arange(N_SX, dtype=jnp.int32) * TILE)[:, None]
        corner_rows = (row_number * TILE + offsets[:, :, 0]).reshape(-1).astype(jnp.int32)
        corner_cols = (column_base + offsets[:, :, 1]).reshape(-1).astype(jnp.int32)
        corners = jnp.stack([corner_rows, corner_cols], axis=1)
        patches = jax.vmap(lambda corner: lax.dynamic_slice(canvas, (jnp.int32(0), corner[0], corner[1]), (2, PATCH, PATCH)))(corners)
        object_real = patches[:, 0]
        object_imag = patches[:, 1]
        back_real, back_imag = back_waves(object_real, object_imag, probe_modes, measured.reshape(-1, PATCH, PATCH))
        grad_real = jnp.sum(probe_real * back_real + probe_imag * back_imag, axis=1)
        grad_imag = jnp.sum(probe_real * back_imag - probe_imag * back_real, axis=1)
        lighting = jnp.broadcast_to(jnp.sum(probe_real * probe_real + probe_imag * probe_imag, axis=1), grad_real.shape)
        terms = jnp.stack([grad_real, grad_imag, lighting], axis=1)
        numer_real = jnp.sum(object_real[:, None] * back_real + object_imag[:, None] * back_imag, axis=0)
        numer_imag = jnp.sum(object_real[:, None] * back_imag - object_imag[:, None] * back_real, axis=0)
        numerator = numerator + jnp.stack([numer_real, numer_imag], axis=1)
        denominator = denominator + jnp.sum(object_real * object_real + object_imag * object_imag, axis=0)

        def place_patch(number, running):
            corner = corners[number]
            existing = lax.dynamic_slice(running, (jnp.int32(0), corner[0], corner[1]), (3, PATCH, PATCH))
            return lax.dynamic_update_slice(running, existing + terms[number], (jnp.int32(0), corner[0], corner[1]))

        gradients = lax.fori_loop(0, corners.shape[0], place_patch, gradients)
        return (gradients, numerator, denominator), None

    start = (jnp.zeros((3,) + canvas.shape[1:], canvas.dtype), jnp.zeros(probe_modes.shape, canvas.dtype), jnp.zeros((PATCH, PATCH), canvas.dtype))
    rows_in = jnp.arange(N_SY, dtype=jnp.int32)
    (gradients, numerator, denominator), unused = lax.scan(row_block, start, (rows_in, scan_offsets, intensities))
    inner = gradients[:, HALF:HALF + OBJ_Y, HALF:HALF + OBJ_X]
    fresh = canvas[:, HALF:HALF + OBJ_Y, HALF:HALF + OBJ_X] - OBJECT_STEP * inner[:2] / (inner[2:3] + REGULAR)
    canvas = canvas.at[:, HALF:HALF + OBJ_Y, HALF:HALF + OBJ_X].set(fresh)
    probe_modes = probe_modes - PROBE_STEP * numerator / (denominator + REGULAR)
    return canvas, probe_modes


def reference(object_tile, probe_modes, scan_offsets, intensities):
    canvas = jnp.pad(object_tile, ((0, 0), (HALF, HALF), (HALF, HALF)))
    for iteration in range(ITERS):
        canvas, probe_modes = one_pass(canvas, probe_modes, scan_offsets, intensities)
    return canvas[:, HALF:HALF + OBJ_Y, HALF:HALF + OBJ_X], probe_modes
```

```python
import functools

import jax
import jax.numpy as jnp
import numpy as np
from jax import lax
from jax.experimental import pallas as pl
from jax.experimental.pallas import tpu as pltpu
from jax.sharding import PartitionSpec as P

ITERS = 2
OBJECT_STEP = 0.5
PROBE_STEP = 2.0
REGULAR = 1.0


def dft_tables(extent):
    line = np.arange(extent)
    angle = (line[:, None] * line[None, :] % extent) * (2.0 * np.pi / extent)
    cosine, sine = np.cos(angle) / np.sqrt(extent), np.sin(angle) / np.sqrt(extent)
    table = np.block([[cosine, -sine], [sine, cosine]])
    high = table.astype(jnp.bfloat16)
    low = (table - high.astype(np.float64)).astype(jnp.bfloat16)
    return np.stack([high, low, high.T, low.T])


def split(values):
    high = values.astype(jnp.bfloat16)
    return high, (values - high.astype(jnp.float32)).astype(jnp.bfloat16)


def product(left, right):
    dot = functools.partial(jnp.dot, preferred_element_type=jnp.float32)
    return dot(left[0], right[0]) + (dot(left[0], right[1]) + dot(left[1], right[0]))


def swapped(values, axis, odd):
    count = lax.axis_size(axis)
    pairs = []
    for first in range(1 if odd else 0, count - 1, 2):
        pairs += [(first, first + 1), (first + 1, first)]
    return lax.ppermute(values, axis, pairs)


def flipped(values, axis, bits):
    return lax.ppermute(values, axis, [(i, i ^ bits) for i in range(lax.axis_size(axis))])


def tree_sum(parts):
    while len(parts) > 1:
        parts = [parts[i] + parts[i + 1] for i in range(0, len(parts), 2)]
    return parts[0]


def scalars_of(offsets, canvas_size, halo):
    row, col = lax.axis_index("sy"), lax.axis_index("sx")
    rows, cols = lax.axis_size("sy"), lax.axis_size("sx")
    head = [
        row % 2,
        col % 2,
        row // 2,
        jnp.where(row == 0, halo, 0),
        jnp.where(row == rows - 1, canvas_size - halo, canvas_size),
        jnp.where(col == 0, halo, 0),
        jnp.where(col == cols - 1, canvas_size - halo, canvas_size),
    ]
    return jnp.concatenate([jnp.stack(head).astype(jnp.int32), offsets.reshape(-1)])


HEAD = 7


def updated_canvas(scal, canvas_ref, sums, store):
    half = canvas_ref.shape[-1]
    for a in range(2):
        row = pl.multiple_of(jnp.where(scal[0] == a, half, 0), half)
        for b in range(2):
            side = jnp.where(scal[1] == b, 1, 0)
            at_row = lax.broadcasted_iota(jnp.int32, (half, half), 0) + row
            at_col = lax.broadcasted_iota(jnp.int32, (half, half), 1) + side * half
            inside = (at_row >= scal[3]) & (at_row < scal[4]) & (at_col >= scal[5]) & (at_col < scal[6])
            scale = jnp.where(inside, OBJECT_STEP / (sums[b][a, 2] + REGULAR), 0.0)
            for part in range(2):
                here = (part, side, pl.ds(row, half))
                store(here, canvas_ref[here] - scale * sums[b][a, part])


def place_probe(scal, own_ref, other_ref, probe_ref):
    chips, planes, rows, _ = own_ref.shape
    for slot in range(chips):
        chunk = scal[2] ^ slot
        for which, ref in ((scal[0], own_ref), (1 - scal[0], other_ref)):
            start = pl.multiple_of((which * chips + chunk) * rows, rows)
            for plane in range(planes):
                probe_ref[plane // 2, plane % 2, pl.ds(start, rows), :] = ref[slot, plane]


def terms_body(scal, canvas_ref, probe_ref, measured_ref, table_ref, grad_out, keep_out, send_out, grad, sums):
    positions, extent, _ = measured_ref.shape
    modes = probe_ref.shape[0]
    w1 = (table_ref[0], table_ref[1])
    w2 = (table_ref[2], table_ref[3])
    grad[...] = jnp.zeros_like(grad)
    lighting = None
    for k in range(modes):
        for part in range(2):
            term = probe_ref[k, part] * probe_ref[k, part]
            lighting = term if lighting is None else lighting + term
    lane = lax.broadcasted_iota(jnp.int32, (extent, extent), 1)
    for j in range(positions):
        row, col = scal[HEAD + 2 * j], scal[HEAD + 2 * j + 1]
        turn = col & (extent - 1)
        back = (extent - col) & (extent - 1)
        o_r, o_i = [
            jnp.where(
                lane < extent - col,
                pltpu.roll(canvas_ref[part, 0, pl.ds(row, extent), :], back, 1),
                pltpu.roll(canvas_ref[part, 1, pl.ds(row, extent), :], back, 1),
            )
            for part in range(2)
        ]
        waves = []
        for k in range(modes):
            p_r, p_i = probe_ref[k, 0], probe_ref[k, 1]
            waves.append(jnp.concatenate([p_r * o_r - p_i * o_i, p_r * o_i + p_i * o_r], axis=1))
        half = product(split(jnp.concatenate(waves, axis=0)), w1)
        rows = [half[k * extent : (k + 1) * extent] for k in range(modes)]
        half = jnp.concatenate(
            [jnp.concatenate([r[:, part * extent : (part + 1) * extent] for r in rows], axis=1) for part in range(2)],
            axis=0,
        )
        spectrum = product(w2, split(half))
        squares = spectrum * spectrum
        power = squares[:extent] + squares[extent:]
        misfit = sum(power[:, k * extent : (k + 1) * extent] for k in range(modes)) - measured_ref[j]
        wide = jnp.concatenate([misfit] * modes, axis=1)
        weighted = spectrum * jnp.concatenate([wide, wide], axis=0)
        half = product(w1, split(weighted))
        half = jnp.concatenate(
            [
                jnp.concatenate([half[:extent, k * extent : (k + 1) * extent], half[extent:, k * extent : (k + 1) * extent]], axis=1)
                for k in range(modes)
            ],
            axis=0,
        )
        chi = product(split(half), w2)
        g_r = g_i = 0.0
        for k in range(modes):
            p_r, p_i = probe_ref[k, 0], probe_ref[k, 1]
            c_r = chi[k * extent : (k + 1) * extent, :extent]
            c_i = chi[k * extent : (k + 1) * extent, extent:]
            g_r = g_r + (p_r * c_r + p_i * c_i)
            g_i = g_i + (p_r * c_i - p_i * c_r)
            for part, term in ((0, o_r * c_r + o_i * c_i), (1, o_r * c_i - o_i * c_r)):
                plane = 2 * k + part
                sums[plane] = term if j == 0 else sums[plane] + term
        term = o_r * o_r + o_i * o_i
        sums[2 * modes] = term if j == 0 else sums[2 * modes] + term
        for plane, term in enumerate((g_r, g_i, lighting)):
            moved = pltpu.roll(term, turn, 1)
            grad[plane, 0, pl.ds(row, extent), :] += jnp.where(lane >= col, moved, 0.0)
            grad[plane, 1, pl.ds(row, extent), :] += jnp.where(lane < col, moved, 0.0)
    for a in range(2):
        row = pl.multiple_of(jnp.where(scal[0] == a, extent, 0), extent)
        for b in range(2):
            side = jnp.where(scal[1] == b, 1, 0)
            for plane in range(3):
                grad_out[a, b, plane] = grad[plane, side, pl.ds(row, extent), :]
    chips, planes, rows, _ = keep_out.shape
    for slot in range(chips):
        chunk = scal[2] ^ slot
        for which, ref in ((scal[0], keep_out), (1 - scal[0], send_out)):
            start = pl.multiple_of((which * chips + chunk) * rows, rows)
            for plane in range(planes):
                ref[slot, plane] = sums[plane, pl.ds(start, rows), :]


def first_kernel(scal, canvas_ref, probe_ref, measured_ref, table_ref, grad_out, keep_out, send_out, grad, sums):
    terms_body(scal, canvas_ref, probe_ref, measured_ref, table_ref, grad_out, keep_out, send_out, grad, sums)


def next_kernel(
    scal, old_ref, sums_a, sums_b, own_ref, other_ref, measured_ref, table_ref,
    grad_out, keep_out, send_out, canvas_ref, grad, sums, probe_ref,
):
    def store(here, values):
        canvas_ref[here] = values

    updated_canvas(scal, old_ref, (sums_a, sums_b), store)
    place_probe(scal, own_ref, other_ref, probe_ref)
    terms_body(scal, canvas_ref, probe_ref, measured_ref, table_ref, grad_out, keep_out, send_out, grad, sums)


def last_kernel(scal, old_ref, sums_a, sums_b, own_ref, other_ref, object_ref, probe_ref, canvas):
    half = old_ref.shape[-1]
    halo = half // 2

    def store(here, values):
        canvas[here] = values

    updated_canvas(scal, old_ref, (sums_a, sums_b), store)
    place_probe(scal, own_ref, other_ref, probe_ref)
    for part in range(2):
        middle = pl.ds(halo, half)
        lane = lax.broadcasted_iota(jnp.int32, (half, half), 1)
        object_ref[part] = jnp.where(
            lane < halo, pltpu.roll(canvas[part, 0, middle, :], halo, 1), pltpu.roll(canvas[part, 1, middle, :], halo, 1)
        )


SMEM = pl.BlockSpec(memory_space=pltpu.SMEM)
VMEM = pl.BlockSpec(memory_space=pltpu.VMEM)
PARAMS = pltpu.CompilerParams(vmem_limit_bytes=32 * 1024 * 1024)


def f32(*shape):
    return jax.ShapeDtypeStruct(shape, jnp.float32)


def fetch(tile, halo):
    def rims(values, axis, dim):
        odd = lax.axis_index(axis) % 2 == 1
        low = lax.slice_in_dim(values, 0, halo, axis=dim)
        high = lax.slice_in_dim(values, values.shape[dim] - halo, None, axis=dim)
        near = swapped(jnp.where(odd, low, high), axis, False)
        far = swapped(jnp.where(odd, high, low), axis, True)
        return jnp.where(odd, near, far), jnp.where(odd, far, near)

    above, below = rims(tile, "sy", 1)
    column = jnp.concatenate([above, tile, below], axis=1)
    left, right = rims(column, "sx", 2)
    return jnp.stack(
        [jnp.concatenate([left, column[..., :-halo]], axis=2), jnp.concatenate([column[..., halo:], right], axis=2)],
        axis=1,
    )


def neighbour_sums(grad):
    near = grad[0] + swapped(grad[0], "sy", False)
    far = grad[1] + swapped(grad[1], "sy", True)
    side_a = jnp.stack([near[0], far[0]])
    side_b = jnp.stack([near[1], far[1]])
    return side_a + swapped(side_a, "sx", False), side_b + swapped(side_b, "sx", True)


def probe_step(probe_chunk, keep, send):
    chips = keep.shape[0]
    planes = probe_chunk.shape[0]
    both = keep + swapped(send, "sy", False)
    total = tree_sum([both[0]] + [flipped(both[t], "sy", 2 * t) for t in range(1, chips)])
    total = tree_sum([total] + [flipped(total, "sx", t) for t in range(1, lax.axis_size("sx"))])
    fresh = probe_chunk - PROBE_STEP * total[:planes] / (total[planes:] + REGULAR)
    own = jnp.stack([fresh] + [flipped(fresh, "sy", 2 * t) for t in range(1, chips)])
    return fresh, own, swapped(own, "sy", False)


def per_device(object_tile, probe_modes, scan_offsets, intensities):
    tile = object_tile.shape[1]
    modes, _, extent, _ = probe_modes.shape
    halo = extent // 2
    size = tile + 2 * halo
    chips = lax.axis_size("sy") // 2
    rows = extent // 2 // chips
    planes = 2 * modes
    measured = intensities[0, 0]
    table = jnp.asarray(dft_tables(extent))
    scal = scalars_of(scan_offsets[0, 0], size, halo)
    outs = (f32(2, 2, 3, tile, tile), f32(chips, planes + 1, rows, extent), f32(chips, planes + 1, rows, extent))
    scratch = [pltpu.VMEM((3, 2, size, tile), jnp.float32), pltpu.VMEM((planes + 1, extent, extent), jnp.float32)]
    canvas = fetch(object_tile, halo)
    start = (lax.axis_index("sy") % 2 * chips + lax.axis_index("sy") // 2) * rows
    chunk = lax.dynamic_slice_in_dim(probe_modes.reshape(planes, extent, extent), start, rows, axis=1)
    grad, keep, send = pl.pallas_call(
        first_kernel,
        out_shape=outs,
        in_specs=[SMEM] + [VMEM] * 4,
        out_specs=[VMEM] * 3,
        scratch_shapes=scratch,
        compiler_params=PARAMS,
    )(scal, canvas, probe_modes, measured, table)
    for iteration in range(1, ITERS):
        sums_a, sums_b = neighbour_sums(grad)
        chunk, own, other = probe_step(chunk, keep, send)
        grad, keep, send, canvas = pl.pallas_call(
            next_kernel,
            out_shape=outs + (f32(2, 2, size, tile),),
            in_specs=[SMEM] + [VMEM] * 7,
            out_specs=[VMEM] * 4,
            scratch_shapes=scratch + [pltpu.VMEM(probe_modes.shape, jnp.float32)],
            compiler_params=PARAMS,
        )(scal, canvas, sums_a, sums_b, own, other, measured, table)
    sums_a, sums_b = neighbour_sums(grad)
    chunk, own, other = probe_step(chunk, keep, send)
    return pl.pallas_call(
        last_kernel,
        out_shape=(f32(2, tile, tile), f32(*probe_modes.shape)),
        in_specs=[SMEM] + [VMEM] * 5,
        out_specs=[VMEM] * 2,
        scratch_shapes=[pltpu.VMEM((2, 2, size, tile), jnp.float32)],
        compiler_params=PARAMS,
    )(scal, canvas, sums_a, sums_b, own, other)


def solution(mesh):
    placed = (P(None, "sy", "sx"), P(), P("sy", "sx", None, None), P("sy", "sx", None, None, None))
    return jax.shard_map(
        per_device,
        mesh=mesh,
        in_specs=placed,
        out_specs=(P(None, "sy", "sx"), P()),
        check_vma=False,
    )
```

```python
import functools

import jax
import jax.numpy as jnp
import numpy as np
from jax import lax
from jax.experimental import pallas as pl
from jax.experimental.pallas import tpu as pltpu
from jax.sharding import PartitionSpec as P

ITERS = 2
OBJECT_STEP = 0.5
PROBE_STEP = 2.0
REGULAR = 1.0


def dft_tables(extent):
    line = np.arange(extent)
    angle = (line[:, None] * line[None, :] % extent) * (2.0 * np.pi / extent)
    cosine, sine = np.cos(angle) / np.sqrt(extent), np.sin(angle) / np.sqrt(extent)
    table = np.block([[cosine, -sine], [sine, cosine]])
    high = table.astype(jnp.bfloat16)
    low = (table - high.astype(np.float64)).astype(jnp.bfloat16)
    return np.stack([high, low, high.T, low.T])


def split(values):
    high = values.astype(jnp.bfloat16)
    return high, (values - high.astype(jnp.float32)).astype(jnp.bfloat16)


def product(left, right):
    dot = functools.partial(jnp.dot, preferred_element_type=jnp.float32)
    return dot(left[0], right[0]) + (dot(left[0], right[1]) + dot(left[1], right[0]))


def swapped(values, axis, odd):
    count = lax.axis_size(axis)
    pairs = []
    for first in range(1 if odd else 0, count - 1, 2):
        pairs += [(first, first + 1), (first + 1, first)]
    return lax.ppermute(values, axis, pairs)


def flipped(values, axis, bits):
    return lax.ppermute(values, axis, [(i, i ^ bits) for i in range(lax.axis_size(axis))])


def tree_sum(parts):
    while len(parts) > 1:
        parts = [parts[i] + parts[i + 1] for i in range(0, len(parts), 2)]
    return parts[0]


def head_scalars(canvas_size, halo):
    row, col = lax.axis_index("sy"), lax.axis_index("sx")
    rows, cols = lax.axis_size("sy"), lax.axis_size("sx")
    head = [
        row % 2,
        col % 2,
        row // 2,
        jnp.where(row == 0, halo, 0),
        jnp.where(row == rows - 1, canvas_size - halo, canvas_size),
        jnp.where(col == 0, halo, 0),
        jnp.where(col == cols - 1, canvas_size - halo, canvas_size),
    ]
    return jnp.stack(head).astype(jnp.int32)


HEAD = 7


def light_kernel(scal, corners, probe_ref, scale_ref, lit):
    _, size, extent = scale_ref.shape
    lit[...] = jnp.zeros_like(lit)
    weight = sum(probe_ref[k, part] * probe_ref[k, part] for k in range(probe_ref.shape[0]) for part in range(2))
    lane = lax.broadcasted_iota(jnp.int32, (extent, extent), 1)

    count = corners.shape[0] // 18
    for device in range(9):
        for j in range(device * count, (device + 1) * count):
            row, col = corners[2 * j] + extent, corners[2 * j + 1]
            moved = pltpu.roll(weight, col & (extent - 1), 1)
            for side in range(2):
                if device % 3 == 2 * (1 - side):
                    continue
                covered = (lane + side * extent >= col) & (lane + side * extent < col + extent)
                lit[side, pl.ds(row, extent), :] += jnp.where(covered, moved, 0.0)
    at_row = lax.broadcasted_iota(jnp.int32, (size, extent), 0)
    at_col = lax.broadcasted_iota(jnp.int32, (size, extent), 1)
    for side in range(2):
        inside = (at_row >= scal[3]) & (at_row < scal[4]) & (at_col + side * extent >= scal[5])
        inside = inside & (at_col + side * extent < scal[6])
        lighting = lit[side, extent : extent + size, :]
        scale_ref[side] = jnp.where(inside, OBJECT_STEP / (lighting + REGULAR), 0.0)


def updated_canvas(scal, old_ref, scale_ref, sums, canvas_ref):
    half = old_ref.shape[-1]
    for a in range(2):
        row = pl.multiple_of(jnp.where(scal[0] == a, half, 0), half)
        for b in range(2):
            side = jnp.where(scal[1] == b, 1, 0)
            scale = scale_ref[side, pl.ds(row, half)]
            for part in range(2):
                here = (part, side, pl.ds(row, half))
                canvas_ref[here] = old_ref[here] - scale * sums[a][b, part]


def place_probe(scal, own_ref, other_ref, probe_ref):
    chips, planes, rows, _ = own_ref.shape
    for slot in range(chips):
        chunk = scal[2] ^ slot
        for which, ref in ((scal[0], own_ref), (1 - scal[0], other_ref)):
            start = pl.multiple_of((which * chips + chunk) * rows, rows)
            for plane in range(planes):
                probe_ref[plane // 2, plane % 2, pl.ds(start, rows), :] = ref[slot, plane]


def terms_body(scal, offs, canvas_ref, probe_ref, measured_ref, table_ref, outs, keep_out, send_out, grad, sums):
    positions, extent, _ = measured_ref.shape
    modes = probe_ref.shape[0]
    w1 = (table_ref[0], table_ref[1])
    w2 = (table_ref[2], table_ref[3])
    grad[...] = jnp.zeros_like(grad)
    lane = lax.broadcasted_iota(jnp.int32, (extent, extent), 1)
    group = positions // 2
    for first in range(0, positions, group):
        span = range(first, min(first + group, positions))
        patches = []
        for j in span:
            row, col = offs[2 * j], offs[2 * j + 1]
            back = (extent - col) & (extent - 1)
            patches.append([
                jnp.where(
                    lane < extent - col,
                    pltpu.roll(canvas_ref[part, 0, pl.ds(row, extent), :], back, 1),
                    pltpu.roll(canvas_ref[part, 1, pl.ds(row, extent), :], back, 1),
                )
                for part in range(2)
            ])
        waves = []
        for o_r, o_i in patches:
            for k in range(modes):
                p_r, p_i = probe_ref[k, 0], probe_ref[k, 1]
                waves.append(jnp.concatenate([p_r * o_r - p_i * o_i, p_r * o_i + p_i * o_r], axis=1))
        count = len(waves)
        half = product(split(jnp.concatenate(waves, axis=0)), w1)
        rows = [half[k * extent : (k + 1) * extent] for k in range(count)]
        half = jnp.concatenate(
            [jnp.concatenate([r[:, part * extent : (part + 1) * extent] for r in rows], axis=1) for part in range(2)],
            axis=0,
        )
        spectrum = product(w2, split(half))
        squares = spectrum * spectrum
        power = squares[:extent] + squares[extent:]
        wide = []
        for at, j in enumerate(span):
            misfit = sum(power[:, k * extent : (k + 1) * extent] for k in range(at * modes, (at + 1) * modes)) - measured_ref[j]
            wide += [misfit] * modes
        wide = jnp.concatenate(wide, axis=1)
        weighted = spectrum * jnp.concatenate([wide, wide], axis=0)
        half = product(w1, split(weighted))
        half = jnp.concatenate(
            [
                jnp.concatenate([half[:extent, k * extent : (k + 1) * extent], half[extent:, k * extent : (k + 1) * extent]], axis=1)
                for k in range(count)
            ],
            axis=0,
        )
        chi = product(split(half), w2)
        for at, j in enumerate(span):
            o_r, o_i = patches[at]
            row, col = offs[2 * j], offs[2 * j + 1]
            turn = col & (extent - 1)
            g_r = g_i = 0.0
            for k in range(modes):
                p_r, p_i = probe_ref[k, 0], probe_ref[k, 1]
                wave = at * modes + k
                c_r = chi[wave * extent : (wave + 1) * extent, :extent]
                c_i = chi[wave * extent : (wave + 1) * extent, extent:]
                g_r = g_r + (p_r * c_r + p_i * c_i)
                g_i = g_i + (p_r * c_i - p_i * c_r)
                for part, term in ((0, o_r * c_r + o_i * c_i), (1, o_r * c_i - o_i * c_r)):
                    plane = 2 * k + part
                    sums[plane] = term if j == 0 else sums[plane] + term
            term = o_r * o_r + o_i * o_i
            sums[2 * modes] = term if j == 0 else sums[2 * modes] + term
            for plane, term in enumerate((g_r, g_i)):
                moved = pltpu.roll(term, turn, 1)
                grad[plane, 0, pl.ds(row, extent), :] += jnp.where(lane >= col, moved, 0.0)
                grad[plane, 1, pl.ds(row, extent), :] += jnp.where(lane < col, moved, 0.0)
    if len(outs) == 1:
        give_quadrants(scal, grad, outs)
    else:
        give_rims(scal, grad, outs)
    chips, planes, rows, _ = keep_out.shape
    for slot in range(chips):
        chunk = scal[2] ^ slot
        for which, ref in ((scal[0], keep_out), (1 - scal[0], send_out)):
            start = pl.multiple_of((which * chips + chunk) * rows, rows)
            for plane in range(planes):
                ref[slot, plane] = sums[plane, pl.ds(start, rows), :]


def give_quadrants(scal, grad, outs):
    extent = grad.shape[-1]
    for a in range(2):
        row = pl.multiple_of(jnp.where(scal[0] == a, extent, 0), extent)
        for b in range(2):
            side = jnp.where(scal[1] == b, 1, 0)
            for plane in range(grad.shape[0]):
                outs[0][b, a, plane] = grad[plane, side, pl.ds(row, extent), :]


def give_rims(scal, grad, outs):
    extent = grad.shape[-1]
    halo = extent // 2
    lane = lax.broadcasted_iota(jnp.int32, (extent, extent), 1)
    for plane in range(grad.shape[0]):
        upper = [grad[plane, side, 0:extent, :] for side in range(2)]
        lower = [grad[plane, side, extent : 2 * extent, :] for side in range(2)]
        for start, rows in ((0, upper), (extent, lower)):
            outs[0][plane, start : start + extent, :] = jnp.where(
                lane < halo, pltpu.roll(rows[0], halo, 1), pltpu.roll(rows[1], halo, 1)
            )
        left = jnp.where(lane < halo, upper[0], pltpu.roll(lower[0], halo, 1))
        right = jnp.where(lane < halo, pltpu.roll(upper[1], halo, 1), lower[1])
        outs[1][1 - scal[1], plane] = left
        outs[1][scal[1], plane] = right


def rim_kernel(scal, own_ref, near_ref, far_ref, middle_ref, near_out, far_out):
    _, size, extent = own_ref.shape
    halo = extent // 2
    lane = lax.broadcasted_iota(jnp.int32, (extent, extent), 1)
    odd = scal[1] == 1
    for plane in range(own_ref.shape[0]):
        near, far = near_ref[plane], far_ref[plane]
        from_left, from_right = jnp.where(odd, near, far), jnp.where(odd, far, near)
        upper = own_ref[plane, 0:extent] + jnp.where(lane < halo, from_left, pltpu.roll(from_right, halo, 1))
        lower = own_ref[plane, extent:size] + jnp.where(lane < halo, pltpu.roll(from_left, halo, 1), from_right)
        middle_ref[plane, 0:halo] = upper[halo:]
        middle_ref[plane, halo:extent] = lower[:halo]
        near_out[plane] = jnp.where(scal[0] == 1, upper[:halo], lower[halo:])
        far_out[plane] = jnp.where(scal[0] == 1, lower[halo:], upper[:halo])


def first_kernel(
    scal, offs, tile_ref, rows_near, rows_far, cols_near, cols_far, probe_ref, measured_ref, table_ref, *rest
):
    outs, (keep_out, send_out, canvas_ref, grad, sums) = rest[:-5], rest[-5:]
    extent = tile_ref.shape[-1]
    halo = extent // 2
    size = 2 * extent
    odd_row, odd_col = scal[0] == 1, scal[1] == 1
    lane = lax.broadcasted_iota(jnp.int32, (extent, extent), 1)
    for part in range(2):
        near, far = (ref[part * halo : (part + 1) * halo] for ref in (rows_near, rows_far))
        above, below = jnp.where(odd_row, near, far), jnp.where(odd_row, far, near)
        for start in range(0, size, extent):
            half = pl.ds(start, extent)
            if start == 0:
                middle = jnp.concatenate([above, tile_ref[part, :halo]], axis=0)
            else:
                middle = jnp.concatenate([tile_ref[part, halo:], below], axis=0)
            middle = pltpu.roll(middle, halo, 1)
            near, far = cols_near[half], cols_far[half]
            if part == 1:
                near, far = pltpu.roll(near, halo, 1), pltpu.roll(far, halo, 1)
            left, right = jnp.where(odd_col, near, far), jnp.where(odd_col, far, near)
            canvas_ref[part, 0, half] = jnp.where(lane < halo, left, middle)
            canvas_ref[part, 1, half] = jnp.where(lane < halo, middle, pltpu.roll(right, halo, 1))
    terms_body(scal, offs, canvas_ref, probe_ref, measured_ref, table_ref, outs, keep_out, send_out, grad, sums)


def next_kernel(scal, offs, old_ref, scale_ref, near_ref, far_ref, own_ref, other_ref, measured_ref, table_ref, *rest):
    outs, (keep_out, send_out, canvas_ref, probe_ref, grad, sums) = rest[:-6], rest[-6:]
    updated_canvas(scal, old_ref, scale_ref, (near_ref, far_ref), canvas_ref)
    place_probe(scal, own_ref, other_ref, probe_ref)
    terms_body(scal, offs, canvas_ref, probe_ref, measured_ref, table_ref, outs, keep_out, send_out, grad, sums)


def last_kernel(scal, old_ref, scale_ref, middle_ref, near_ref, far_ref, own_ref, other_ref, object_ref, probe_ref):
    half = old_ref.shape[-1]
    halo = half // 2
    place_probe(scal, own_ref, other_ref, probe_ref)
    lane = lax.broadcasted_iota(jnp.int32, (half, half), 1)
    middle = pl.ds(halo, half)

    def tile_of(sides):
        return jnp.where(lane < halo, pltpu.roll(sides[0], halo, 1), pltpu.roll(sides[1], halo, 1))

    scale = tile_of([scale_ref[side, middle] for side in range(2)])
    odd = scal[0] == 1
    for part in range(2):
        near, far = near_ref[part], far_ref[part]
        from_rows = jnp.concatenate([jnp.where(odd, near, far), jnp.where(odd, far, near)], axis=0)
        old = tile_of([old_ref[part, side, middle] for side in range(2)])
        object_ref[part] = old - scale * (middle_ref[part] + from_rows)


SMEM = pl.BlockSpec(memory_space=pltpu.SMEM)
VMEM = pl.BlockSpec(memory_space=pltpu.VMEM)
PARAMS = pltpu.CompilerParams(vmem_limit_bytes=32 * 1024 * 1024)


def f32(*shape):
    return jax.ShapeDtypeStruct(shape, jnp.float32)


def kernel_call(body, outs, operands, scratch=(), scalars=2, flops=0):
    return pl.pallas_call(
        body,
        out_shape=outs,
        in_specs=[SMEM] * scalars + [VMEM] * (len(operands) - scalars),
        out_specs=jax.tree.map(lambda _: VMEM, outs),
        scratch_shapes=[pltpu.VMEM(shape, jnp.float32) for shape in scratch],
        compiler_params=PARAMS,
        cost_estimate=pl.CostEstimate(flops=flops, bytes_accessed=1 << 20, transcendentals=0),
    )(*operands)


def fetch(tile, offsets, halo):
    lanes = tile.shape[-1]
    odd_row, odd_col = (lax.axis_index(axis) % 2 == 1 for axis in ("sy", "sx"))
    corners = jnp.pad((offsets.reshape(1, -1) + 1).astype(jnp.float32), ((0, 7), (0, lanes - offsets.size)))

    def rows_of(rim):
        return jnp.concatenate([rim.reshape(-1, lanes), corners])

    upper, lower = tile[:, :halo], tile[:, -halo:]
    rows_near = swapped(rows_of(jnp.where(odd_row, upper, lower)), "sy", False)
    rows_far = swapped(rows_of(jnp.where(odd_row, lower, upper)), "sy", True)
    last = 2 * halo
    above, below = jnp.where(odd_row, rows_near, rows_far), jnp.where(odd_row, rows_far, rows_near)
    column = jnp.concatenate([above[:last].reshape(2, halo, lanes), tile, below[:last].reshape(2, halo, lanes)], axis=1)
    reach = jnp.concatenate([above[last : last + 1], corners[:1], below[last : last + 1], corners[3:]])

    def columns_of(rim):
        return jnp.concatenate([jnp.concatenate([rim[0], rim[1]], axis=1), reach])

    left, right = column[..., :halo], column[..., -halo:]
    cols_near = swapped(columns_of(jnp.where(odd_col, left, right)), "sx", False)
    cols_far = swapped(columns_of(jnp.where(odd_col, right, left)), "sx", True)
    sides = [jnp.where(odd_col, cols_near, cols_far), reach, jnp.where(odd_col, cols_far, cols_near)]
    found = jnp.stack([side[-8:-5, : offsets.size] for side in sides], axis=1).astype(jnp.int32) - 1
    found = found.reshape(3, 3, -1, 2)
    step = (jnp.arange(3, dtype=jnp.int32) - 1) * lanes
    shift = jnp.stack(jnp.broadcast_arrays(step[:, None], step[None, :]), axis=-1)[:, :, None]
    return rows_near, rows_far, cols_near, cols_far, jnp.where(found < 0, -lanes, found + shift).reshape(-1)


def after(value, *others):
    return lax.optimization_barrier((value, *others))[0]


def chip_sum(both):
    return tree_sum([both[0]] + [flipped(both[t], "sy", 2 * t) for t in range(1, both.shape[0])])


def probe_fresh(total, chunk):
    planes = chunk.shape[0]
    total = tree_sum([total] + [flipped(total, "sx", t) for t in range(1, lax.axis_size("sx"))])
    return chunk - PROBE_STEP * total[:planes] / (total[planes:] + REGULAR)


def probe_spread(fresh, chips):
    own = jnp.stack([fresh] + [flipped(fresh, "sy", 2 * t) for t in range(1, chips)])
    return own, swapped(own, "sy", False)


def per_device(object_tile, probe_modes, scan_offsets, intensities):
    tile = object_tile.shape[1]
    modes, _, extent, _ = probe_modes.shape
    halo = extent // 2
    size = tile + 2 * halo
    chips = lax.axis_size("sy") // 2
    rows = extent // 2 // chips
    planes = 2 * modes
    measured = intensities[0, 0]
    table = jnp.asarray(dft_tables(extent))
    scal = head_scalars(size, halo)
    offsets = scan_offsets[0, 0]
    offs = offsets.reshape(-1)
    probe_outs = (f32(chips, planes + 1, rows, extent),) * 2 + (f32(2, 2, size, tile),)
    quadrants = (f32(2, 2, 2, tile, tile),)
    rims = (f32(2, size, tile), f32(2, 2, tile, tile))
    scratch = ((2, 2, size, tile), (planes + 1, extent, extent))
    work = 2 * 3 * offsets.shape[0] * 4 * (2 * extent) ** 3

    start = (lax.axis_index("sy") % 2 * chips + lax.axis_index("sy") // 2) * rows
    chunk = lax.dynamic_slice_in_dim(probe_modes.reshape(planes, extent, extent), start, rows, axis=1)
    *halos, corners = fetch(object_tile, offsets, halo)

    def light(probe, corners):
        lit = (2, 2 * size, extent)
        return kernel_call(light_kernel, f32(2, size, tile), (scal, corners, probe), [lit], flops=work // 2)

    probe = probe_modes
    for iteration in range(ITERS):
        final = iteration == ITERS - 1
        outs = (rims if final else quadrants) + probe_outs
        if iteration == 0:
            operands = (scal, offs, object_tile, *halos, probe, measured, table)
            *given, keep, send, canvas = kernel_call(first_kernel, outs, operands, scratch, flops=work)
        else:
            operands = (scal, offs, canvas, scale, near, far, own, other, measured, table)
            outs = outs + (f32(*probe.shape),)
            *given, keep, send, canvas, probe = kernel_call(next_kernel, outs, operands, scratch, flops=work)
        both = keep + swapped(send, "sy", False)
        scale = light(probe, after(corners, both))
        if not final:
            (grad,) = given
            side_a = grad[0] + swapped(grad[0], "sx", False)
            side_b = grad[1] + swapped(grad[1], "sx", True)
            near, far = jnp.stack([side_a[0], side_b[0]]), jnp.stack([side_a[1], side_b[1]])
            total = after(chip_sum(both), near, far, scale)
            near = near + swapped(near, "sy", False)
            far = far + swapped(far, "sy", True)
            chunk = after(probe_fresh(total, chunk), near, far)
        else:
            own_columns, side = given
            near, far = swapped(side[0], "sx", False), swapped(side[1], "sx", True)
            total = after(chip_sum(both), near, far, scale)
            middle, near, far = kernel_call(
                rim_kernel, (f32(2, tile, tile),) + (f32(2, halo, tile),) * 2, (scal, own_columns, near, far), scalars=1
            )
            near, far = swapped(near, "sy", False), swapped(far, "sy", True)
            chunk = after(probe_fresh(total, chunk), near, far)
        own, other = probe_spread(chunk, chips)
    outs = (f32(2, tile, tile), f32(*probe.shape))
    return kernel_call(last_kernel, outs, (scal, canvas, scale, middle, near, far, own, other), scalars=1)


def solution(mesh):
    placed = (P(None, "sy", "sx"), P(), P("sy", "sx", None, None), P("sy", "sx", None, None, None))
    return jax.shard_map(
        per_device,
        mesh=mesh,
        in_specs=placed,
        out_specs=(P(None, "sy", "sx"), P()),
        check_vma=False,
    )
```

```python
import functools

import jax
import jax.numpy as jnp
import numpy as np
from jax import lax
from jax.experimental import pallas as pl
from jax.experimental.pallas import tpu as pltpu
from jax.sharding import PartitionSpec as P

ITERS = 2
OBJECT_STEP = 0.5
PROBE_STEP = 2.0
REGULAR = 1.0


def dft_tables(extent):
    line = np.arange(extent)
    angle = (line[:, None] * line[None, :] % extent) * (2.0 * np.pi / extent)
    cosine, sine = np.cos(angle) / np.sqrt(extent), np.sin(angle) / np.sqrt(extent)
    table = np.block([[cosine, -sine], [sine, cosine]])
    high = table.astype(jnp.bfloat16)
    low = (table - high.astype(np.float64)).astype(jnp.bfloat16)
    return np.stack([high, low, high.T, low.T])


def split(values):
    high = values.astype(jnp.bfloat16)
    return high, (values - high.astype(jnp.float32)).astype(jnp.bfloat16)


def product(left, right):
    dot = functools.partial(jnp.dot, preferred_element_type=jnp.float32)
    return dot(left[0], right[0]) + (dot(left[0], right[1]) + dot(left[1], right[0]))


def swapped(values, axis, odd):
    count = lax.axis_size(axis)
    pairs = []
    for first in range(1 if odd else 0, count - 1, 2):
        pairs += [(first, first + 1), (first + 1, first)]
    return lax.ppermute(values, axis, pairs)


def flipped(values, axis, bits):
    return lax.ppermute(values, axis, [(i, i ^ bits) for i in range(lax.axis_size(axis))])


def tree_sum(parts):
    while len(parts) > 1:
        parts = [parts[i] + parts[i + 1] for i in range(0, len(parts), 2)]
    return parts[0]


def head_scalars(canvas_size, halo):
    row, col = lax.axis_index("sy"), lax.axis_index("sx")
    rows, cols = lax.axis_size("sy"), lax.axis_size("sx")
    head = [
        row % 2,
        col % 2,
        row // 2,
        jnp.where(row == 0, halo, 0),
        jnp.where(row == rows - 1, canvas_size - halo, canvas_size),
        jnp.where(col == 0, halo, 0),
        jnp.where(col == cols - 1, canvas_size - halo, canvas_size),
    ]
    return jnp.stack(head).astype(jnp.int32)


HEAD = 7


def light_kernel(scal, corners, probe_ref, scale_ref, lit):
    _, size, extent = scale_ref.shape
    lit[...] = jnp.zeros_like(lit)
    weight = sum(probe_ref[k, part] * probe_ref[k, part] for k in range(probe_ref.shape[0]) for part in range(2))
    lane = lax.broadcasted_iota(jnp.int32, (extent, extent), 1)

    count = corners.shape[0] // 18
    for device in range(9):
        for j in range(device * count, (device + 1) * count):
            row, col = corners[2 * j] + extent, corners[2 * j + 1]
            moved = pltpu.roll(weight, col & (extent - 1), 1)
            for side in range(2):
                if device % 3 == 2 * (1 - side):
                    continue
                covered = (lane + side * extent >= col) & (lane + side * extent < col + extent)
                lit[side, pl.ds(row, extent), :] += jnp.where(covered, moved, 0.0)
    at_row = lax.broadcasted_iota(jnp.int32, (size, extent), 0)
    at_col = lax.broadcasted_iota(jnp.int32, (size, extent), 1)
    for side in range(2):
        inside = (at_row >= scal[3]) & (at_row < scal[4]) & (at_col + side * extent >= scal[5])
        inside = inside & (at_col + side * extent < scal[6])
        lighting = lit[side, extent : extent + size, :]
        scale_ref[side] = jnp.where(inside, OBJECT_STEP / (lighting + REGULAR), 0.0)


def updated_canvas(scal, old_ref, scale_ref, sums, canvas_ref):
    half = old_ref.shape[-1]
    for a in range(2):
        row = pl.multiple_of(jnp.where(scal[0] == a, half, 0), half)
        for b in range(2):
            side = jnp.where(scal[1] == b, 1, 0)
            scale = scale_ref[side, pl.ds(row, half)]
            for part in range(2):
                here = (part, side, pl.ds(row, half))
                canvas_ref[here] = old_ref[here] - scale * sums[a][b, part]


def place_probe(scal, own_ref, other_ref, probe_ref):
    chips, planes, rows, _ = own_ref.shape
    for slot in range(chips):
        chunk = scal[2] ^ slot
        for which, ref in ((scal[0], own_ref), (1 - scal[0], other_ref)):
            start = pl.multiple_of((which * chips + chunk) * rows, rows)
            for plane in range(planes):
                probe_ref[plane // 2, plane % 2, pl.ds(start, rows), :] = ref[slot, plane]


def terms_body(scal, offs, canvas_ref, probe_ref, measured_ref, table_ref, outs, keep_out, send_out, grad, sums):
    positions, extent, _ = measured_ref.shape
    modes = probe_ref.shape[0]
    w1 = (table_ref[0], table_ref[1])
    w2 = (table_ref[2], table_ref[3])
    grad[...] = jnp.zeros_like(grad)
    lane = lax.broadcasted_iota(jnp.int32, (extent, extent), 1)
    group = positions // 2
    for first in range(0, positions, group):
        span = range(first, min(first + group, positions))
        patches = []
        for j in span:
            row, col = offs[2 * j], offs[2 * j + 1]
            back = (extent - col) & (extent - 1)
            patches.append([
                jnp.where(
                    lane < extent - col,
                    pltpu.roll(canvas_ref[part, 0, pl.ds(row, extent), :], back, 1),
                    pltpu.roll(canvas_ref[part, 1, pl.ds(row, extent), :], back, 1),
                )
                for part in range(2)
            ])
        waves = []
        for o_r, o_i in patches:
            for k in range(modes):
                p_r, p_i = probe_ref[k, 0], probe_ref[k, 1]
                waves.append(jnp.concatenate([p_r * o_r - p_i * o_i, p_r * o_i + p_i * o_r], axis=1))
        count = len(waves)
        half = product(split(jnp.concatenate(waves, axis=0)), w1)
        rows = [half[k * extent : (k + 1) * extent] for k in range(count)]
        half = jnp.concatenate(
            [jnp.concatenate([r[:, part * extent : (part + 1) * extent] for r in rows], axis=1) for part in range(2)],
            axis=0,
        )
        spectrum = product(w2, split(half))
        squares = spectrum * spectrum
        power = squares[:extent] + squares[extent:]
        wide = []
        for at, j in enumerate(span):
            misfit = sum(power[:, k * extent : (k + 1) * extent] for k in range(at * modes, (at + 1) * modes)) - measured_ref[j]
            wide += [misfit] * modes
        wide = jnp.concatenate(wide, axis=1)
        weighted = spectrum * jnp.concatenate([wide, wide], axis=0)
        half = product(w1, split(weighted))
        half = jnp.concatenate(
            [
                jnp.concatenate([half[:extent, k * extent : (k + 1) * extent], half[extent:, k * extent : (k + 1) * extent]], axis=1)
                for k in range(count)
            ],
            axis=0,
        )
        chi = product(split(half), w2)
        for at, j in enumerate(span):
            o_r, o_i = patches[at]
            row, col = offs[2 * j], offs[2 * j + 1]
            turn = col & (extent - 1)
            g_r = g_i = 0.0
            for k in range(modes):
                p_r, p_i = probe_ref[k, 0], probe_ref[k, 1]
                wave = at * modes + k
                c_r = chi[wave * extent : (wave + 1) * extent, :extent]
                c_i = chi[wave * extent : (wave + 1) * extent, extent:]
                g_r = g_r + (p_r * c_r + p_i * c_i)
                g_i = g_i + (p_r * c_i - p_i * c_r)
                for part, term in ((0, o_r * c_r + o_i * c_i), (1, o_r * c_i - o_i * c_r)):
                    plane = 2 * k + part
                    sums[plane] = term if j == 0 else sums[plane] + term
            term = o_r * o_r + o_i * o_i
            sums[2 * modes] = term if j == 0 else sums[2 * modes] + term
            for plane, term in enumerate((g_r, g_i)):
                moved = pltpu.roll(term, turn, 1)
                grad[plane, 0, pl.ds(row, extent), :] += jnp.where(lane >= col, moved, 0.0)
                grad[plane, 1, pl.ds(row, extent), :] += jnp.where(lane < col, moved, 0.0)
    if len(outs) == 1:
        give_quadrants(scal, grad, outs)
    else:
        give_rims(scal, grad, outs, send_out)
    chips, planes, rows, _ = keep_out.shape
    for slot in range(chips):
        chunk = scal[2] ^ slot
        for which, ref in ((scal[0], keep_out), (1 - scal[0], send_out)):
            start = pl.multiple_of((which * chips + chunk) * rows, rows)
            for plane in range(planes):
                piece = sums[plane, pl.ds(start, rows), :]
                if len(ref.shape) == 2:
                    at = (slot * planes + plane) * rows
                    ref[at : at + rows, :] = piece
                else:
                    ref[slot, plane] = piece


def give_quadrants(scal, grad, outs):
    extent = grad.shape[-1]
    for a in range(2):
        row = pl.multiple_of(jnp.where(scal[0] == a, extent, 0), extent)
        for b in range(2):
            side = jnp.where(scal[1] == b, 1, 0)
            for plane in range(grad.shape[0]):
                outs[0][b, a, plane] = grad[plane, side, pl.ds(row, extent), :]


def give_rims(scal, grad, outs, send_out):
    planes, sides, size, extent = grad.shape
    halo = extent // 2
    base = send_out.shape[0] - planes * sides * halo
    outer = (pl.multiple_of(jnp.where(scal[0] == 1, 0, size - halo), halo), pl.multiple_of(jnp.where(scal[0] == 1, size - halo, 0), halo))
    for plane in range(planes):
        for side in range(sides):
            at = (plane * sides + side) * halo
            outs[0][plane, side] = grad[plane, side, halo : size - halo, :]
            send_out[base + at : base + at + halo, :] = grad[plane, side, pl.ds(outer[0], halo), :]
            outs[1][at : at + halo, :] = grad[plane, side, pl.ds(outer[1], halo), :]


def middle_kernel(scal, own_ref, near_ref, far_ref, total_ref, middle_ref, near_out, far_out):
    planes, sides, extent, _ = own_ref.shape
    halo = extent // 2
    base = near_ref.shape[0] - planes * sides * halo
    head = total_ref.shape[0]
    odd_row, odd_col = scal[0] == 1, scal[1] == 1
    lane = lax.broadcasted_iota(jnp.int32, (extent, extent), 1)
    rims = []
    for plane in range(planes):
        rows = []
        for side in range(sides):
            at = (plane * sides + side) * halo
            near, far = near_ref[base + at : base + at + halo, :], far_ref[at : at + halo, :]
            other = jnp.concatenate([jnp.where(odd_row, near, far), jnp.where(odd_row, far, near)], axis=0)
            rows.append(own_ref[plane, side] + other)
        turned = [pltpu.roll(part, halo, 1) for part in rows]
        middle_ref[plane] = jnp.where(lane < halo, turned[0], turned[1])
        rims.append((rows[0], turned[1]) if plane == 0 else (turned[0], rows[1]))
    left, right = (jnp.where(lane < halo, rims[0][side], rims[1][side]) for side in range(sides))
    for ref, rim in ((near_out, jnp.where(odd_col, left, right)), (far_out, jnp.where(odd_col, right, left))):
        ref[:head, :] = total_ref[...]
        ref[head:, :] = rim


def object_kernel(scal, old_ref, scale_ref, middle_ref, near_ref, far_ref, object_ref):
    extent = old_ref.shape[-1]
    halo = extent // 2
    lane = lax.broadcasted_iota(jnp.int32, (extent, extent), 1)
    middle = pl.ds(halo, extent)

    def tile_of(sides):
        return jnp.where(lane < halo, pltpu.roll(sides[0], halo, 1), pltpu.roll(sides[1], halo, 1))

    scale = tile_of([scale_ref[side, middle] for side in range(2)])
    odd = scal[1] == 1
    near, far = (ref[ref.shape[0] - extent :, :] for ref in (near_ref, far_ref))
    left = jnp.where(scal[5] > 0, 0.0, jnp.where(odd, near, far))
    right = jnp.where(scal[6] < 2 * extent, 0.0, jnp.where(odd, far, near))
    for part in range(2):
        if part == 0:
            beside = jnp.where(lane < halo, left, pltpu.roll(right, halo, 1))
        else:
            beside = jnp.where(lane < halo, pltpu.roll(left, halo, 1), right)
        old = tile_of([old_ref[part, side, middle] for side in range(2)])
        object_ref[part] = old - scale * (middle_ref[part] + beside)


def first_kernel(
    scal, offs, tile_ref, rows_near, rows_far, cols_near, cols_far, probe_ref, measured_ref, table_ref, *rest
):
    outs, (keep_out, send_out, canvas_ref, grad, sums) = rest[:-5], rest[-5:]
    extent = tile_ref.shape[-1]
    halo = extent // 2
    size = 2 * extent
    odd_row, odd_col = scal[0] == 1, scal[1] == 1
    lane = lax.broadcasted_iota(jnp.int32, (extent, extent), 1)
    for part in range(2):
        near, far = (ref[part * halo : (part + 1) * halo] for ref in (rows_near, rows_far))
        above, below = jnp.where(odd_row, near, far), jnp.where(odd_row, far, near)
        for start in range(0, size, extent):
            half = pl.ds(start, extent)
            if start == 0:
                middle = jnp.concatenate([above, tile_ref[part, :halo]], axis=0)
            else:
                middle = jnp.concatenate([tile_ref[part, halo:], below], axis=0)
            middle = pltpu.roll(middle, halo, 1)
            near, far = cols_near[half], cols_far[half]
            if part == 1:
                near, far = pltpu.roll(near, halo, 1), pltpu.roll(far, halo, 1)
            left, right = jnp.where(odd_col, near, far), jnp.where(odd_col, far, near)
            canvas_ref[part, 0, half] = jnp.where(lane < halo, left, middle)
            canvas_ref[part, 1, half] = jnp.where(lane < halo, middle, pltpu.roll(right, halo, 1))
    terms_body(scal, offs, canvas_ref, probe_ref, measured_ref, table_ref, outs, keep_out, send_out, grad, sums)


def next_kernel(scal, offs, old_ref, scale_ref, near_ref, far_ref, own_ref, other_ref, measured_ref, table_ref, *rest):
    outs, (keep_out, send_out, canvas_ref, probe_ref, grad, sums) = rest[:-6], rest[-6:]
    updated_canvas(scal, old_ref, scale_ref, (near_ref, far_ref), canvas_ref)
    place_probe(scal, own_ref, other_ref, probe_ref)
    terms_body(scal, offs, canvas_ref, probe_ref, measured_ref, table_ref, outs, keep_out, send_out, grad, sums)


def last_kernel(scal, own_ref, other_ref, probe_ref):
    place_probe(scal, own_ref, other_ref, probe_ref)


SMEM = pl.BlockSpec(memory_space=pltpu.SMEM)
VMEM = pl.BlockSpec(memory_space=pltpu.VMEM)
PARAMS = pltpu.CompilerParams(vmem_limit_bytes=32 * 1024 * 1024)


def f32(*shape):
    return jax.ShapeDtypeStruct(shape, jnp.float32)


def kernel_call(body, outs, operands, scratch=(), scalars=2, flops=0):
    return pl.pallas_call(
        body,
        out_shape=outs,
        in_specs=[SMEM] * scalars + [VMEM] * (len(operands) - scalars),
        out_specs=jax.tree.map(lambda _: VMEM, outs),
        scratch_shapes=[pltpu.VMEM(shape, jnp.float32) for shape in scratch],
        compiler_params=PARAMS,
        cost_estimate=pl.CostEstimate(flops=flops, bytes_accessed=1 << 20, transcendentals=0),
    )(*operands)


def fetch(tile, offsets, halo):
    lanes = tile.shape[-1]
    odd_row, odd_col = (lax.axis_index(axis) % 2 == 1 for axis in ("sy", "sx"))
    corners = jnp.pad((offsets.reshape(1, -1) + 1).astype(jnp.float32), ((0, 7), (0, lanes - offsets.size)))

    def rows_of(rim):
        return jnp.concatenate([rim.reshape(-1, lanes), corners])

    upper, lower = tile[:, :halo], tile[:, -halo:]
    rows_near = swapped(rows_of(jnp.where(odd_row, upper, lower)), "sy", False)
    rows_far = swapped(rows_of(jnp.where(odd_row, lower, upper)), "sy", True)
    last = 2 * halo
    above, below = jnp.where(odd_row, rows_near, rows_far), jnp.where(odd_row, rows_far, rows_near)
    column = jnp.concatenate([above[:last].reshape(2, halo, lanes), tile, below[:last].reshape(2, halo, lanes)], axis=1)
    reach = jnp.concatenate([above[last : last + 1], corners[:1], below[last : last + 1], corners[3:]])

    def columns_of(rim):
        return jnp.concatenate([jnp.concatenate([rim[0], rim[1]], axis=1), reach])

    left, right = column[..., :halo], column[..., -halo:]
    cols_near = swapped(columns_of(jnp.where(odd_col, left, right)), "sx", False)
    cols_far = swapped(columns_of(jnp.where(odd_col, right, left)), "sx", True)
    sides = [jnp.where(odd_col, cols_near, cols_far), reach, jnp.where(odd_col, cols_far, cols_near)]
    found = jnp.stack([side[-8:-5, : offsets.size] for side in sides], axis=1).astype(jnp.int32) - 1
    found = found.reshape(3, 3, -1, 2)
    step = (jnp.arange(3, dtype=jnp.int32) - 1) * lanes
    shift = jnp.stack(jnp.broadcast_arrays(step[:, None], step[None, :]), axis=-1)[:, :, None]
    return rows_near, rows_far, cols_near, cols_far, jnp.where(found < 0, -lanes, found + shift).reshape(-1)


def after(value, *others):
    return lax.optimization_barrier((value, *others))[0]


def chip_sum(both):
    return tree_sum([both[0]] + [flipped(both[t], "sy", 2 * t) for t in range(1, both.shape[0])])


def probe_fresh(parts, chunk):
    planes, rows, lanes = chunk.shape
    total = tree_sum(parts).reshape(planes + 1, rows, lanes)
    return chunk - PROBE_STEP * total[:planes] / (total[planes:] + REGULAR)


def across(total, start):
    return [total] + [flipped(total, "sx", t) for t in range(start, lax.axis_size("sx"))]


def probe_spread(fresh, chips):
    return jnp.stack([fresh] + [flipped(fresh, "sy", 2 * t) for t in range(1, chips)])


def per_device(object_tile, probe_modes, scan_offsets, intensities):
    tile = object_tile.shape[1]
    modes, _, extent, _ = probe_modes.shape
    halo = extent // 2
    size = tile + 2 * halo
    chips = lax.axis_size("sy") // 2
    rows = extent // 2 // chips
    planes = 2 * modes
    measured = intensities[0, 0]
    table = jnp.asarray(dft_tables(extent))
    scal = head_scalars(size, halo)
    offsets = scan_offsets[0, 0]
    offs = offsets.reshape(-1)
    kept = (chips, planes + 1, rows, extent)
    count = chips * (planes + 1) * rows
    rim_rows = 2 * 2 * halo
    quadrants = (f32(2, 2, 2, tile, tile),)
    rims = (f32(2, 2, tile, tile), f32(rim_rows, tile))
    scratch = ((2, 2, size, tile), (planes + 1, extent, extent))
    work = 2 * 3 * offsets.shape[0] * 4 * (2 * extent) ** 3

    start = (lax.axis_index("sy") % 2 * chips + lax.axis_index("sy") // 2) * rows
    chunk = lax.dynamic_slice_in_dim(probe_modes.reshape(planes, extent, extent), start, rows, axis=1)
    *halos, corners = fetch(object_tile, offsets, halo)

    def light(probe, corners):
        lit = (2, 2 * size, extent)
        return kernel_call(light_kernel, f32(2, size, tile), (scal, corners, probe), [lit], flops=work // 2)

    probe = probe_modes
    for iteration in range(ITERS):
        final = iteration == ITERS - 1
        sent = (count + rim_rows, extent) if final else kept
        outs = (rims if final else quadrants) + (f32(*kept), f32(*sent), f32(2, 2, size, tile))
        if iteration == 0:
            operands = (scal, offs, object_tile, *halos, probe, measured, table)
            *given, keep, send, canvas = kernel_call(first_kernel, outs, operands, scratch, flops=work)
        else:
            operands = (scal, offs, canvas, scale, near, far, own, other, measured, table)
            outs = outs + (f32(*probe.shape),)
            *given, keep, send, canvas, probe = kernel_call(next_kernel, outs, operands, scratch, flops=work)
        received = swapped(send, "sy", False)
        both = keep + received.reshape(-1, extent)[:count].reshape(kept)
        scale = light(probe, after(corners, both))
        if not final:
            (grad,) = given
            side_a = grad[0] + swapped(grad[0], "sx", False)
            side_b = grad[1] + swapped(grad[1], "sx", True)
            near, far = jnp.stack([side_a[0], side_b[0]]), jnp.stack([side_a[1], side_b[1]])
            near = near + swapped(near, "sy", False)
            far = far + swapped(far, "sy", True)
            total = after(chip_sum(both), near, scale)
            chunk = after(probe_fresh(across(total, 1), chunk), near, far)
        else:
            own_rows, far = given
            far = swapped(far, "sy", True)
            total = after(chip_sum(both), far, scale).reshape(-1, extent)
            message = f32(total.shape[0] + tile, tile)
            middle, near, far = kernel_call(
                middle_kernel, (f32(2, tile, tile), message, message), (scal, own_rows, received, far, total), scalars=1
            )
            near = flipped(near, "sx", 1)
            head = total.shape[0]
            if lax.axis_size("sx") == 4:
                far = flipped(far, "sx", 3)
                parts = [total, near[:head], flipped(total, "sx", 2), far[:head]]
            else:
                far = swapped(far, "sx", True)
                parts = across(total, 2)
                parts.insert(1, near[:head])
            chunk = probe_fresh(parts, chunk)
            outcome = kernel_call(object_kernel, f32(2, tile, tile), (scal, canvas, scale, middle, near, far), scalars=1)
        own = probe_spread(chunk, chips)
        other = swapped(after(own, outcome) if final else own, "sy", False)
    return outcome, kernel_call(last_kernel, f32(*probe.shape), (scal, own, other), scalars=1)


def solution(mesh):
    placed = (P(None, "sy", "sx"), P(), P("sy", "sx", None, None), P("sy", "sx", None, None, None))
    return jax.shard_map(
        per_device,
        mesh=mesh,
        in_specs=placed,
        out_specs=(P(None, "sy", "sx"), P()),
        check_vma=False,
    )
```

```python
import functools

import jax
import jax.numpy as jnp
import numpy as np
from jax import lax
from jax.experimental import pallas as pl
from jax.experimental.pallas import tpu as pltpu
from jax.sharding import PartitionSpec as P

ITERS = 2
OBJECT_STEP = 0.5
PROBE_STEP = 2.0
REGULAR = 1.0


def dft_tables(extent):
    line = np.arange(extent)
    angle = (line[:, None] * line[None, :] % extent) * (2.0 * np.pi / extent)
    cosine, sine = np.cos(angle) / np.sqrt(extent), np.sin(angle) / np.sqrt(extent)
    table = np.block([[cosine, -sine], [sine, cosine]])
    high = table.astype(jnp.bfloat16)
    low = (table - high.astype(np.float64)).astype(jnp.bfloat16)
    return np.stack([high, low, high.T, low.T])


def split(values):
    high = values.astype(jnp.bfloat16)
    return high, (values - high.astype(jnp.float32)).astype(jnp.bfloat16)


def product(left, right):
    dot = functools.partial(jnp.dot, preferred_element_type=jnp.float32)
    return dot(left[0], right[0]) + (dot(left[0], right[1]) + dot(left[1], right[0]))


def swapped(values, axis, odd):
    count = lax.axis_size(axis)
    pairs = []
    for first in range(1 if odd else 0, count - 1, 2):
        pairs += [(first, first + 1), (first + 1, first)]
    return lax.ppermute(values, axis, pairs)


def flipped(values, axis, bits):
    return lax.ppermute(values, axis, [(i, i ^ bits) for i in range(lax.axis_size(axis))])


def tree_sum(parts):
    while len(parts) > 1:
        parts = [parts[i] + parts[i + 1] for i in range(0, len(parts), 2)]
    return parts[0]


def head_scalars(canvas_size, halo):
    row, col = lax.axis_index("sy"), lax.axis_index("sx")
    rows, cols = lax.axis_size("sy"), lax.axis_size("sx")
    head = [
        row % 2,
        col % 2,
        row // 2,
        jnp.where(row == 0, halo, 0),
        jnp.where(row == rows - 1, canvas_size - halo, canvas_size),
        jnp.where(col == 0, halo, 0),
        jnp.where(col == cols - 1, canvas_size - halo, canvas_size),
    ]
    return jnp.stack(head).astype(jnp.int32)


HEAD = 7


def light_kernel(scal, corners, probe_ref, scale_ref, lit):
    _, size, extent = scale_ref.shape
    lit[...] = jnp.zeros_like(lit)
    weight = sum(probe_ref[k, part] * probe_ref[k, part] for k in range(probe_ref.shape[0]) for part in range(2))
    lane = lax.broadcasted_iota(jnp.int32, (extent, extent), 1)

    for device in range(corners.shape[0]):
        for j in range(corners.shape[2]):
            row, col = corners[device, 0, j] + extent, corners[device, 1, j]
            moved = pltpu.roll(weight, col & (extent - 1), 1)
            for side in range(2):
                if device % 3 == 2 * (1 - side):
                    continue
                covered = (lane + side * extent >= col) & (lane + side * extent < col + extent)
                lit[side, pl.ds(row, extent), :] += jnp.where(covered, moved, 0.0)
    at_row = lax.broadcasted_iota(jnp.int32, (size, extent), 0)
    at_col = lax.broadcasted_iota(jnp.int32, (size, extent), 1)
    for side in range(2):
        inside = (at_row >= scal[3]) & (at_row < scal[4]) & (at_col + side * extent >= scal[5])
        inside = inside & (at_col + side * extent < scal[6])
        lighting = lit[side, extent : extent + size, :]
        scale_ref[side] = jnp.where(inside, OBJECT_STEP / (lighting + REGULAR), 0.0)


def updated_canvas(scal, old_ref, scale_ref, sums, canvas_ref):
    half = old_ref.shape[-1]
    for a in range(2):
        row = pl.multiple_of(jnp.where(scal[0] == a, half, 0), half)
        for b in range(2):
            side = jnp.where(scal[1] == b, 1, 0)
            scale = scale_ref[side, pl.ds(row, half)]
            for part in range(2):
                here = (part, side, pl.ds(row, half))
                canvas_ref[here] = old_ref[here] - scale * sums[a][b, part]


def place_probe(scal, own_ref, other_ref, probe_ref):
    chips, planes, rows, _ = own_ref.shape
    for slot in range(chips):
        chunk = scal[2] ^ slot
        for which, ref in ((scal[0], own_ref), (1 - scal[0], other_ref)):
            start = pl.multiple_of((which * chips + chunk) * rows, rows)
            for plane in range(planes):
                probe_ref[plane // 2, plane % 2, pl.ds(start, rows), :] = ref[slot, plane]


def terms_body(scal, offs, canvas_ref, probe_ref, measured_ref, table_ref, outs, keep_out, send_out, grad, sums):
    positions, extent, _ = measured_ref.shape
    modes = probe_ref.shape[0]
    w1 = (table_ref[0], table_ref[1])
    w2 = (table_ref[2], table_ref[3])
    grad[...] = jnp.zeros_like(grad)
    lane = lax.broadcasted_iota(jnp.int32, (extent, extent), 1)
    group = positions // 2
    for first in range(0, positions, group):
        span = range(first, min(first + group, positions))
        patches = []
        for j in span:
            row, col = offs[0, j], offs[1, j]
            back = (extent - col) & (extent - 1)
            patches.append([
                jnp.where(
                    lane < extent - col,
                    pltpu.roll(canvas_ref[part, 0, pl.ds(row, extent), :], back, 1),
                    pltpu.roll(canvas_ref[part, 1, pl.ds(row, extent), :], back, 1),
                )
                for part in range(2)
            ])
        waves = []
        for o_r, o_i in patches:
            for k in range(modes):
                p_r, p_i = probe_ref[k, 0], probe_ref[k, 1]
                waves.append(jnp.concatenate([p_r * o_r - p_i * o_i, p_r * o_i + p_i * o_r], axis=1))
        count = len(waves)
        half = product(split(jnp.concatenate(waves, axis=0)), w1)
        rows = [half[k * extent : (k + 1) * extent] for k in range(count)]
        half = jnp.concatenate(
            [jnp.concatenate([r[:, part * extent : (part + 1) * extent] for r in rows], axis=1) for part in range(2)],
            axis=0,
        )
        spectrum = product(w2, split(half))
        squares = spectrum * spectrum
        power = squares[:extent] + squares[extent:]
        wide = []
        for at, j in enumerate(span):
            misfit = sum(power[:, k * extent : (k + 1) * extent] for k in range(at * modes, (at + 1) * modes)) - measured_ref[j]
            wide += [misfit] * modes
        wide = jnp.concatenate(wide, axis=1)
        weighted = spectrum * jnp.concatenate([wide, wide], axis=0)
        half = product(w1, split(weighted))
        half = jnp.concatenate(
            [
                jnp.concatenate([half[:extent, k * extent : (k + 1) * extent], half[extent:, k * extent : (k + 1) * extent]], axis=1)
                for k in range(count)
            ],
            axis=0,
        )
        chi = product(split(half), w2)
        for at, j in enumerate(span):
            o_r, o_i = patches[at]
            row, col = offs[0, j], offs[1, j]
            turn = col & (extent - 1)
            g_r = g_i = 0.0
            for k in range(modes):
                p_r, p_i = probe_ref[k, 0], probe_ref[k, 1]
                wave = at * modes + k
                c_r = chi[wave * extent : (wave + 1) * extent, :extent]
                c_i = chi[wave * extent : (wave + 1) * extent, extent:]
                g_r = g_r + (p_r * c_r + p_i * c_i)
                g_i = g_i + (p_r * c_i - p_i * c_r)
                for part, term in ((0, o_r * c_r + o_i * c_i), (1, o_r * c_i - o_i * c_r)):
                    plane = 2 * k + part
                    sums[plane] = term if j == 0 else sums[plane] + term
            term = o_r * o_r + o_i * o_i
            sums[2 * modes] = term if j == 0 else sums[2 * modes] + term
            for plane, term in enumerate((g_r, g_i)):
                moved = pltpu.roll(term, turn, 1)
                grad[plane, 0, pl.ds(row, extent), :] += jnp.where(lane >= col, moved, 0.0)
                grad[plane, 1, pl.ds(row, extent), :] += jnp.where(lane < col, moved, 0.0)
    if len(outs[0].shape) == len(outs[1].shape):
        give_quadrants(scal, grad, outs)
    else:
        give_rims(scal, grad, outs, send_out)
    chips, planes, rows, _ = keep_out.shape
    for slot in range(chips):
        chunk = scal[2] ^ slot
        for which, ref in ((scal[0], keep_out), (1 - scal[0], send_out)):
            start = pl.multiple_of((which * chips + chunk) * rows, rows)
            for plane in range(planes):
                piece = sums[plane, pl.ds(start, rows), :]
                if len(ref.shape) == 2:
                    at = (slot * planes + plane) * rows
                    ref[at : at + rows, :] = piece
                else:
                    ref[slot, plane] = piece


def give_quadrants(scal, grad, outs):
    extent = grad.shape[-1]
    for a in range(2):
        row = pl.multiple_of(jnp.where(scal[0] == a, extent, 0), extent)
        for b in range(2):
            side = jnp.where(scal[1] == b, 1, 0)
            for plane in range(grad.shape[0]):
                outs[b][a, plane] = grad[plane, side, pl.ds(row, extent), :]


def give_rims(scal, grad, outs, send_out):
    planes, sides, size, extent = grad.shape
    halo = extent // 2
    base = send_out.shape[0] - planes * sides * halo
    outer = (pl.multiple_of(jnp.where(scal[0] == 1, 0, size - halo), halo), pl.multiple_of(jnp.where(scal[0] == 1, size - halo, 0), halo))
    for plane in range(planes):
        for side in range(sides):
            at = (plane * sides + side) * halo
            outs[0][plane, side] = grad[plane, side, halo : size - halo, :]
            send_out[base + at : base + at + halo, :] = grad[plane, side, pl.ds(outer[0], halo), :]
            outs[1][at : at + halo, :] = grad[plane, side, pl.ds(outer[1], halo), :]


def middle_kernel(scal, own_ref, near_ref, far_ref, total_ref, middle_ref, near_out, far_out):
    planes, sides, extent, _ = own_ref.shape
    halo = extent // 2
    base = near_ref.shape[0] - planes * sides * halo
    head = total_ref.shape[0]
    odd_row, odd_col = scal[0] == 1, scal[1] == 1
    lane = lax.broadcasted_iota(jnp.int32, (extent, extent), 1)
    rims = []
    for plane in range(planes):
        rows = []
        for side in range(sides):
            at = (plane * sides + side) * halo
            near, far = near_ref[base + at : base + at + halo, :], far_ref[at : at + halo, :]
            other = jnp.concatenate([jnp.where(odd_row, near, far), jnp.where(odd_row, far, near)], axis=0)
            rows.append(own_ref[plane, side] + other)
        turned = [pltpu.roll(part, halo, 1) for part in rows]
        middle_ref[plane] = jnp.where(lane < halo, turned[0], turned[1])
        rims.append((rows[0], turned[1]) if plane == 0 else (turned[0], rows[1]))
    left, right = (jnp.where(lane < halo, rims[0][side], rims[1][side]) for side in range(sides))
    for ref, rim in ((near_out, jnp.where(odd_col, left, right)), (far_out, jnp.where(odd_col, right, left))):
        ref[:head, :] = total_ref[...]
        ref[head:, :] = rim


def object_kernel(scal, old_ref, scale_ref, middle_ref, near_ref, far_ref, object_ref):
    extent = old_ref.shape[-1]
    halo = extent // 2
    lane = lax.broadcasted_iota(jnp.int32, (extent, extent), 1)
    middle = pl.ds(halo, extent)

    def tile_of(sides):
        return jnp.where(lane < halo, pltpu.roll(sides[0], halo, 1), pltpu.roll(sides[1], halo, 1))

    scale = tile_of([scale_ref[side, middle] for side in range(2)])
    odd = scal[1] == 1
    near, far = (ref[ref.shape[0] - extent :, :] for ref in (near_ref, far_ref))
    left = jnp.where(scal[5] > 0, 0.0, jnp.where(odd, near, far))
    right = jnp.where(scal[6] < 2 * extent, 0.0, jnp.where(odd, far, near))
    for part in range(2):
        if part == 0:
            beside = jnp.where(lane < halo, left, pltpu.roll(right, halo, 1))
        else:
            beside = jnp.where(lane < halo, pltpu.roll(left, halo, 1), right)
        old = tile_of([old_ref[part, side, middle] for side in range(2)])
        object_ref[part] = old - scale * (middle_ref[part] + beside)


def first_kernel(
    scal, offs, tile_ref, rows_near, rows_far, cols_near, cols_far, reach, probe_ref, measured_ref, table_ref,
    reaches_out, *rest,
):
    reaches_out[0:8, :], reaches_out[8:16, :], reaches_out[16:24, :] = cols_near[-8:, :], cols_far[-8:, :], reach[...]
    outs, (keep_out, send_out, canvas_ref, grad, sums) = rest[:-5], rest[-5:]
    extent = tile_ref.shape[-1]
    halo = extent // 2
    size = 2 * extent
    odd_row, odd_col = scal[0] == 1, scal[1] == 1
    lane = lax.broadcasted_iota(jnp.int32, (extent, extent), 1)
    for part in range(2):
        near, far = (ref[part * halo : (part + 1) * halo] for ref in (rows_near, rows_far))
        above, below = jnp.where(odd_row, near, far), jnp.where(odd_row, far, near)
        for start in range(0, size, extent):
            half = pl.ds(start, extent)
            if start == 0:
                middle = jnp.concatenate([above, tile_ref[part, :halo]], axis=0)
            else:
                middle = jnp.concatenate([tile_ref[part, halo:], below], axis=0)
            middle = pltpu.roll(middle, halo, 1)
            near, far = cols_near[half], cols_far[half]
            if part == 1:
                near, far = pltpu.roll(near, halo, 1), pltpu.roll(far, halo, 1)
            left, right = jnp.where(odd_col, near, far), jnp.where(odd_col, far, near)
            canvas_ref[part, 0, half] = jnp.where(lane < halo, left, middle)
            canvas_ref[part, 1, half] = jnp.where(lane < halo, middle, pltpu.roll(right, halo, 1))
    terms_body(scal, offs, canvas_ref, probe_ref, measured_ref, table_ref, outs, keep_out, send_out, grad, sums)


def next_kernel(scal, offs, old_ref, scale_ref, near_ref, far_ref, own_ref, other_ref, measured_ref, table_ref, *rest):
    outs, (keep_out, send_out, canvas_ref, probe_ref, grad, sums) = rest[:-6], rest[-6:]
    updated_canvas(scal, old_ref, scale_ref, (near_ref, far_ref), canvas_ref)
    place_probe(scal, own_ref, other_ref, probe_ref)
    terms_body(scal, offs, canvas_ref, probe_ref, measured_ref, table_ref, outs, keep_out, send_out, grad, sums)


def last_kernel(scal, own_ref, other_ref, probe_ref):
    place_probe(scal, own_ref, other_ref, probe_ref)


SMEM = pl.BlockSpec(memory_space=pltpu.SMEM)
VMEM = pl.BlockSpec(memory_space=pltpu.VMEM)
PARAMS = pltpu.CompilerParams(vmem_limit_bytes=32 * 1024 * 1024)


def f32(*shape):
    return jax.ShapeDtypeStruct(shape, jnp.float32)


def kernel_call(body, outs, operands, scratch=(), scalars=2, flops=0):
    return pl.pallas_call(
        body,
        out_shape=outs,
        in_specs=[SMEM] * scalars + [VMEM] * (len(operands) - scalars),
        out_specs=jax.tree.map(lambda _: VMEM, outs),
        scratch_shapes=[pltpu.VMEM(shape, jnp.float32) for shape in scratch],
        compiler_params=PARAMS,
        cost_estimate=pl.CostEstimate(flops=flops, bytes_accessed=1 << 20, transcendentals=0),
    )(*operands)


def fetch(tile, offs, halo):
    lanes = tile.shape[-1]
    odd_row, odd_col = (lax.axis_index(axis) % 2 == 1 for axis in ("sy", "sx"))
    upper, lower = tile[:, :halo].reshape(-1, lanes), tile[:, halo:].reshape(-1, lanes)
    near, far = jnp.where(odd_row, upper, lower), jnp.where(odd_row, lower, upper)
    own = jnp.pad((after(offs, near, far) + 1).astype(jnp.float32), ((0, 6), (0, lanes - offs.shape[1])))
    near, far = jnp.concatenate([near, own]), jnp.concatenate([far, own])
    rows_near, rows_far = swapped(near, "sy", False), swapped(far, "sy", True)
    side = after(tile, near, far)
    left = jnp.concatenate([side[0, :, :halo], side[1, :, :halo]], axis=1)
    right = jnp.concatenate([side[0, :, halo:], side[1, :, halo:]], axis=1)
    left, right = jnp.where(odd_col, left, right), jnp.where(odd_col, right, left)
    above, below = jnp.where(odd_row, rows_near, rows_far), jnp.where(odd_row, rows_far, rows_near)
    last = 2 * halo
    reach = jnp.concatenate([above[last : last + 2], own[:2], below[last : last + 2], own[6:]])

    def columns_of(middle, first):
        ends = []
        for rim in (above, below):
            rim = rim[:last].reshape(2, halo, lanes)
            half = [jnp.where(first, rim[part, :, :halo], rim[part, :, halo:]) for part in range(2)]
            ends.append(jnp.concatenate(half, axis=1))
        return jnp.concatenate([ends[0], middle, ends[1], reach])

    cols_near = swapped(columns_of(left, odd_col), "sx", False)
    cols_far = swapped(columns_of(right, ~odd_col), "sx", True)
    return rows_near, rows_far, cols_near, cols_far, reach


def corners_of(reaches, positions, extent):
    near, far, own = reaches[:8], reaches[8:16], reaches[16:]
    odd = lax.axis_index("sx") % 2 == 1
    sides = [jnp.where(odd, near, far), own, jnp.where(odd, far, near)]
    found = jnp.stack([side[:6, :positions].reshape(3, 2, positions) for side in sides], axis=1)
    found = found.reshape(9, 2, positions).astype(jnp.int32) - 1
    at = jnp.arange(9, dtype=jnp.int32)
    step = (jnp.stack([at // 3, at % 3], axis=1) - 1) * extent
    return jnp.where(found < 0, -extent, found + step[:, :, None])


def after(value, *others):
    return lax.optimization_barrier((value, *others))[0]


def chip_sum(both):
    return tree_sum([both[0]] + [flipped(both[t], "sy", 2 * t) for t in range(1, both.shape[0])])


def probe_fresh(parts, chunk):
    planes, rows, lanes = chunk.shape
    total = tree_sum(parts).reshape(planes + 1, rows, lanes)
    return chunk - PROBE_STEP * total[:planes] / (total[planes:] + REGULAR)


def across(total, start):
    return [total] + [flipped(total, "sx", t) for t in range(start, lax.axis_size("sx"))]


def probe_spread(fresh, chips):
    return jnp.stack([fresh] + [flipped(fresh, "sy", 2 * t) for t in range(1, chips)])


def per_device(object_tile, probe_modes, scan_offsets, intensities):
    tile = object_tile.shape[1]
    modes, _, extent, _ = probe_modes.shape
    halo = extent // 2
    size = tile + 2 * halo
    chips = lax.axis_size("sy") // 2
    rows = extent // 2 // chips
    planes = 2 * modes
    measured = intensities[0, 0]
    table = jnp.asarray(dft_tables(extent))
    scal = head_scalars(size, halo)
    offsets = scan_offsets[0, 0]
    positions = offsets.shape[0]
    offs = offsets.T
    kept = (chips, planes + 1, rows, extent)
    count = chips * (planes + 1) * rows
    rim_rows = 2 * 2 * halo
    quadrants = (f32(2, 2, tile, tile),) * 2
    rims = (f32(2, 2, tile, tile), f32(rim_rows, tile))
    scratch = ((2, 2, size, tile), (planes + 1, extent, extent))
    work = 2 * 3 * positions * 4 * (2 * extent) ** 3

    start = (lax.axis_index("sy") % 2 * chips + lax.axis_index("sy") // 2) * rows
    chunk = lax.dynamic_slice_in_dim(probe_modes.reshape(planes, extent, extent), start, rows, axis=1)
    halos = fetch(object_tile, offs, halo)

    def light(probe, corners):
        lit = (2, 2 * size, extent)
        return kernel_call(light_kernel, f32(2, size, tile), (scal, corners, probe), [lit], flops=work // 2)

    probe = probe_modes
    for iteration in range(ITERS):
        final = iteration == ITERS - 1
        sent = (count + rim_rows, extent) if final else kept
        outs = (rims if final else quadrants) + (f32(*kept), f32(*sent), f32(2, 2, size, tile))
        if iteration == 0:
            operands = (scal, offs, object_tile, *halos, probe, measured, table)
            outs = (f32(24, tile),) + outs
            reaches, *given, keep, send, canvas = kernel_call(first_kernel, outs, operands, scratch, flops=work)
        else:
            operands = (scal, offs, canvas, scale, near, far, own, other, measured, table)
            outs = outs + (f32(*probe.shape),)
            *given, keep, send, canvas, probe = kernel_call(next_kernel, outs, operands, scratch, flops=work)
        received = swapped(send, "sy", False)
        both = keep + received.reshape(-1, extent)[:count].reshape(kept)
        if iteration == 0:
            corners = corners_of(after(reaches, both), positions, tile)
        scale = light(probe, after(corners, both))
        if not final:
            side_a = given[0] + swapped(given[0], "sx", False)
            side_b = given[1] + swapped(given[1], "sx", True)
            near, far = jnp.stack([side_a[0], side_b[0]]), jnp.stack([side_a[1], side_b[1]])
            near = near + swapped(near, "sy", False)
            far = far + swapped(far, "sy", True)
            total = after(chip_sum(both), near, scale)
            chunk = after(probe_fresh(across(total, 1), chunk), near, far)
        else:
            own_rows, far = given
            far = swapped(far, "sy", True)
            total = after(chip_sum(both), far, scale).reshape(-1, extent)
            message = f32(total.shape[0] + tile, tile)
            middle, near, far = kernel_call(
                middle_kernel, (f32(2, tile, tile), message, message), (scal, own_rows, received, far, total), scalars=1
            )
            head = total.shape[0]
            near = flipped(near, "sx", 1)
            far = swapped(far[head:], "sx", True)
            parts = across(total, 2)
            parts.insert(1, near[:head])
            chunk = probe_fresh(parts, chunk)
            outcome = kernel_call(object_kernel, f32(2, tile, tile), (scal, canvas, scale, middle, near, far), scalars=1)
        own = probe_spread(chunk, chips)
        other = swapped(after(own, outcome) if final else own, "sy", False)
    return outcome, kernel_call(last_kernel, f32(*probe.shape), (scal, own, other), scalars=1)


def solution(mesh):
    placed = (P(None, "sy", "sx"), P(), P("sy", "sx", None, None), P("sy", "sx", None, None, None))
    return jax.shard_map(
        per_device,
        mesh=mesh,
        in_specs=placed,
        out_specs=(P(None, "sy", "sx"), P()),
        check_vma=False,
    )
```

```python
import functools

import jax
import jax.numpy as jnp
import numpy as np
from jax import lax
from jax.experimental import pallas as pl
from jax.experimental.pallas import tpu as pltpu
from jax.sharding import PartitionSpec as P

ITERS = 2
OBJECT_STEP = 0.5
PROBE_STEP = 2.0
REGULAR = 1.0


def dft_tables(extent):
    line = np.arange(extent)
    angle = (line[:, None] * line[None, :] % extent) * (2.0 * np.pi / extent)
    cosine, sine = np.cos(angle) / np.sqrt(extent), np.sin(angle) / np.sqrt(extent)
    table = np.block([[cosine, -sine], [sine, cosine]])
    high = table.astype(jnp.bfloat16)
    low = (table - high.astype(np.float64)).astype(jnp.bfloat16)
    return np.stack([high, low, high.T, low.T])


def split(values):
    high = values.astype(jnp.bfloat16)
    return high, (values - high.astype(jnp.float32)).astype(jnp.bfloat16)


def product(left, right):
    dot = functools.partial(jnp.dot, preferred_element_type=jnp.float32)
    return dot(left[0], right[0]) + (dot(left[0], right[1]) + dot(left[1], right[0]))


def swapped(values, axis, odd):
    if not odd:
        return lax.ppermute(values, axis, [(i, i ^ 1) for i in range(lax.axis_size(axis))])
    rows, cols = lax.axis_size("sy"), lax.axis_size("sx")
    pairs = []
    for row in range(rows):
        for col in range(cols):
            to_row, to_col = row, col
            if axis == "sy":
                to_row = (row + 1 if row % 2 else row - 1) % rows
            elif 0 < col < cols - 1:
                to_col = col + 1 if col % 2 else col - 1
            else:
                to_row = row ^ 1
            pairs.append((row * cols + col, to_row * cols + to_col))
    return lax.ppermute(values, ("sy", "sx"), pairs)


def partnered(received, axis):
    at = lax.axis_index(axis)
    return jnp.where((at == 0) | (at == lax.axis_size(axis) - 1), 0.0, received)


def flipped(values, axis, bits):
    return lax.ppermute(values, axis, [(i, i ^ bits) for i in range(lax.axis_size(axis))])


def tree_sum(parts):
    while len(parts) > 1:
        parts = [parts[i] + parts[i + 1] for i in range(0, len(parts), 2)]
    return parts[0]


def head_scalars(canvas_size, halo):
    row, col = lax.axis_index("sy"), lax.axis_index("sx")
    rows, cols = lax.axis_size("sy"), lax.axis_size("sx")
    head = [
        row % 2,
        col % 2,
        row // 2,
        jnp.where(row == 0, halo, 0),
        jnp.where(row == rows - 1, canvas_size - halo, canvas_size),
        jnp.where(col == 0, halo, 0),
        jnp.where(col == cols - 1, canvas_size - halo, canvas_size),
    ]
    return jnp.stack(head).astype(jnp.int32)


HEAD = 7


def light_kernel(scal, corners, probe_ref, scale_ref, lit):
    _, size, extent = scale_ref.shape
    lit[...] = jnp.zeros_like(lit)
    weight = sum(probe_ref[k, part] * probe_ref[k, part] for k in range(probe_ref.shape[0]) for part in range(2))
    lane = lax.broadcasted_iota(jnp.int32, (extent, extent), 1)

    for device in range(corners.shape[0]):
        for j in range(corners.shape[2]):
            row, col = corners[device, 0, j] + extent, corners[device, 1, j]
            moved = pltpu.roll(weight, col & (extent - 1), 1)
            for side in range(2):
                if device % 3 == 2 * (1 - side):
                    continue
                covered = (lane + side * extent >= col) & (lane + side * extent < col + extent)
                lit[side, pl.ds(row, extent), :] += jnp.where(covered, moved, 0.0)
    at_row = lax.broadcasted_iota(jnp.int32, (size, extent), 0)
    at_col = lax.broadcasted_iota(jnp.int32, (size, extent), 1)
    for side in range(2):
        inside = (at_row >= scal[3]) & (at_row < scal[4]) & (at_col + side * extent >= scal[5])
        inside = inside & (at_col + side * extent < scal[6])
        lighting = lit[side, extent : extent + size, :]
        scale_ref[side] = jnp.where(inside, OBJECT_STEP / (lighting + REGULAR), 0.0)


def updated_canvas(scal, old_ref, scale_ref, sums, canvas_ref):
    half = old_ref.shape[-1]
    for a in range(2):
        row = pl.multiple_of(jnp.where(scal[0] == a, half, 0), half)
        for b in range(2):
            side = jnp.where(scal[1] == b, 1, 0)
            scale = scale_ref[side, pl.ds(row, half)]
            for part in range(2):
                here = (part, side, pl.ds(row, half))
                canvas_ref[here] = old_ref[here] - scale * sums[a][b, part]


def place_probe(scal, own_ref, other_ref, probe_ref):
    chips, planes, rows, _ = own_ref.shape
    for slot in range(chips):
        chunk = scal[2] ^ slot
        for which, ref in ((scal[0], own_ref), (1 - scal[0], other_ref)):
            start = pl.multiple_of((which * chips + chunk) * rows, rows)
            for plane in range(planes):
                probe_ref[plane // 2, plane % 2, pl.ds(start, rows), :] = ref[slot, plane]


def terms_body(scal, offs, canvas_ref, probe_ref, measured_ref, table_ref, outs, keep_out, send_out, grad, sums):
    positions, extent, _ = measured_ref.shape
    modes = probe_ref.shape[0]
    w1 = (table_ref[0], table_ref[1])
    w2 = (table_ref[2], table_ref[3])
    grad[...] = jnp.zeros_like(grad)
    lane = lax.broadcasted_iota(jnp.int32, (extent, extent), 1)
    group = positions // 2
    for first in range(0, positions, group):
        span = range(first, min(first + group, positions))
        patches = []
        for j in span:
            row, col = offs[0, j], offs[1, j]
            back = (extent - col) & (extent - 1)
            patches.append([
                jnp.where(
                    lane < extent - col,
                    pltpu.roll(canvas_ref[part, 0, pl.ds(row, extent), :], back, 1),
                    pltpu.roll(canvas_ref[part, 1, pl.ds(row, extent), :], back, 1),
                )
                for part in range(2)
            ])
        waves = []
        for o_r, o_i in patches:
            for k in range(modes):
                p_r, p_i = probe_ref[k, 0], probe_ref[k, 1]
                waves.append(jnp.concatenate([p_r * o_r - p_i * o_i, p_r * o_i + p_i * o_r], axis=1))
        count = len(waves)
        half = product(split(jnp.concatenate(waves, axis=0)), w1)
        rows = [half[k * extent : (k + 1) * extent] for k in range(count)]
        half = jnp.concatenate(
            [jnp.concatenate([r[:, part * extent : (part + 1) * extent] for r in rows], axis=1) for part in range(2)],
            axis=0,
        )
        spectrum = product(w2, split(half))
        squares = spectrum * spectrum
        power = squares[:extent] + squares[extent:]
        wide = []
        for at, j in enumerate(span):
            misfit = sum(power[:, k * extent : (k + 1) * extent] for k in range(at * modes, (at + 1) * modes)) - measured_ref[j]
            wide += [misfit] * modes
        wide = jnp.concatenate(wide, axis=1)
        weighted = spectrum * jnp.concatenate([wide, wide], axis=0)
        half = product(w1, split(weighted))
        half = jnp.concatenate(
            [
                jnp.concatenate([half[:extent, k * extent : (k + 1) * extent], half[extent:, k * extent : (k + 1) * extent]], axis=1)
                for k in range(count)
            ],
            axis=0,
        )
        chi = product(split(half), w2)
        for at, j in enumerate(span):
            o_r, o_i = patches[at]
            row, col = offs[0, j], offs[1, j]
            turn = col & (extent - 1)
            g_r = g_i = 0.0
            for k in range(modes):
                p_r, p_i = probe_ref[k, 0], probe_ref[k, 1]
                wave = at * modes + k
                c_r = chi[wave * extent : (wave + 1) * extent, :extent]
                c_i = chi[wave * extent : (wave + 1) * extent, extent:]
                g_r = g_r + (p_r * c_r + p_i * c_i)
                g_i = g_i + (p_r * c_i - p_i * c_r)
                for part, term in ((0, o_r * c_r + o_i * c_i), (1, o_r * c_i - o_i * c_r)):
                    plane = 2 * k + part
                    sums[plane] = term if j == 0 else sums[plane] + term
            term = o_r * o_r + o_i * o_i
            sums[2 * modes] = term if j == 0 else sums[2 * modes] + term
            for plane, term in enumerate((g_r, g_i)):
                moved = pltpu.roll(term, turn, 1)
                grad[plane, 0, pl.ds(row, extent), :] += jnp.where(lane >= col, moved, 0.0)
                grad[plane, 1, pl.ds(row, extent), :] += jnp.where(lane < col, moved, 0.0)
    if len(outs[0].shape) == len(outs[1].shape):
        give_quadrants(scal, grad, outs)
    else:
        give_rims(scal, grad, outs, send_out)
    chips, planes, rows, _ = keep_out.shape
    for slot in range(chips):
        chunk = scal[2] ^ slot
        for which, ref in ((scal[0], keep_out), (1 - scal[0], send_out)):
            start = pl.multiple_of((which * chips + chunk) * rows, rows)
            for plane in range(planes):
                piece = sums[plane, pl.ds(start, rows), :]
                if len(ref.shape) == 2:
                    at = (slot * planes + plane) * rows
                    ref[at : at + rows, :] = piece
                else:
                    ref[slot, plane] = piece


def give_quadrants(scal, grad, outs):
    extent = grad.shape[-1]
    for a in range(2):
        row = pl.multiple_of(jnp.where(scal[0] == a, extent, 0), extent)
        for b in range(2):
            side = jnp.where(scal[1] == b, 1, 0)
            for plane in range(grad.shape[0]):
                outs[b][a, plane] = grad[plane, side, pl.ds(row, extent), :]


def give_rims(scal, grad, outs, send_out):
    planes, sides, size, extent = grad.shape
    halo = extent // 2
    base = send_out.shape[0] - planes * sides * halo
    outer = (pl.multiple_of(jnp.where(scal[0] == 1, 0, size - halo), halo), pl.multiple_of(jnp.where(scal[0] == 1, size - halo, 0), halo))
    for plane in range(planes):
        for side in range(sides):
            at = (plane * sides + side) * halo
            outs[0][plane, side] = grad[plane, side, halo : size - halo, :]
            send_out[base + at : base + at + halo, :] = grad[plane, side, pl.ds(outer[0], halo), :]
            outs[1][at : at + halo, :] = grad[plane, side, pl.ds(outer[1], halo), :]


def middle_kernel(scal, own_ref, near_ref, far_ref, total_ref, middle_ref, near_out, far_out):
    planes, sides, extent, _ = own_ref.shape
    halo = extent // 2
    base = near_ref.shape[0] - planes * sides * halo
    head = total_ref.shape[0]
    odd_row, odd_col = scal[0] == 1, scal[1] == 1
    lane = lax.broadcasted_iota(jnp.int32, (extent, extent), 1)
    rims = []
    for plane in range(planes):
        rows = []
        for side in range(sides):
            at = (plane * sides + side) * halo
            near, far = near_ref[base + at : base + at + halo, :], far_ref[at : at + halo, :]
            other = jnp.concatenate([jnp.where(odd_row, near, far), jnp.where(odd_row, far, near)], axis=0)
            rows.append(own_ref[plane, side] + other)
        turned = [pltpu.roll(part, halo, 1) for part in rows]
        middle_ref[plane] = jnp.where(lane < halo, turned[0], turned[1])
        rims.append((rows[0], turned[1]) if plane == 0 else (turned[0], rows[1]))
    left, right = (jnp.where(lane < halo, rims[0][side], rims[1][side]) for side in range(sides))
    for ref, rim in ((near_out, jnp.where(odd_col, left, right)), (far_out, jnp.where(odd_col, right, left))):
        ref[:head, :] = total_ref[...]
        ref[head:, :] = rim


def object_kernel(scal, old_ref, scale_ref, middle_ref, near_ref, far_ref, object_ref):
    extent = old_ref.shape[-1]
    halo = extent // 2
    lane = lax.broadcasted_iota(jnp.int32, (extent, extent), 1)
    middle = pl.ds(halo, extent)

    def tile_of(sides):
        return jnp.where(lane < halo, pltpu.roll(sides[0], halo, 1), pltpu.roll(sides[1], halo, 1))

    scale = tile_of([scale_ref[side, middle] for side in range(2)])
    odd = scal[1] == 1
    near, far = (ref[ref.shape[0] - extent :, :] for ref in (near_ref, far_ref))
    left = jnp.where(scal[5] > 0, 0.0, jnp.where(odd, near, far))
    right = jnp.where(scal[6] < 2 * extent, 0.0, jnp.where(odd, far, near))
    for part in range(2):
        if part == 0:
            beside = jnp.where(lane < halo, left, pltpu.roll(right, halo, 1))
        else:
            beside = jnp.where(lane < halo, pltpu.roll(left, halo, 1), right)
        old = tile_of([old_ref[part, side, middle] for side in range(2)])
        object_ref[part] = old - scale * (middle_ref[part] + beside)


def first_kernel(
    scal, offs, tile_ref, rows_near, rows_far, cols_near, cols_far, reach, probe_ref, measured_ref, table_ref,
    reaches_out, *rest,
):
    reaches_out[0:8, :], reaches_out[8:16, :], reaches_out[16:24, :] = cols_near[-8:, :], cols_far[-8:, :], reach[...]
    outs, (keep_out, send_out, canvas_ref, grad, sums) = rest[:-5], rest[-5:]
    extent = tile_ref.shape[-1]
    halo = extent // 2
    size = 2 * extent
    odd_row, odd_col = scal[0] == 1, scal[1] == 1
    lane = lax.broadcasted_iota(jnp.int32, (extent, extent), 1)
    for part in range(2):
        near, far = (ref[part * halo : (part + 1) * halo] for ref in (rows_near, rows_far))
        above, below = jnp.where(odd_row, near, far), jnp.where(odd_row, far, near)
        for start in range(0, size, extent):
            half = pl.ds(start, extent)
            if start == 0:
                middle = jnp.concatenate([above, tile_ref[part, :halo]], axis=0)
            else:
                middle = jnp.concatenate([tile_ref[part, halo:], below], axis=0)
            middle = pltpu.roll(middle, halo, 1)
            near, far = cols_near[half], cols_far[half]
            if part == 1:
                near, far = pltpu.roll(near, halo, 1), pltpu.roll(far, halo, 1)
            left, right = jnp.where(odd_col, near, far), jnp.where(odd_col, far, near)
            canvas_ref[part, 0, half] = jnp.where(lane < halo, left, middle)
            canvas_ref[part, 1, half] = jnp.where(lane < halo, middle, pltpu.roll(right, halo, 1))
    terms_body(scal, offs, canvas_ref, probe_ref, measured_ref, table_ref, outs, keep_out, send_out, grad, sums)


def next_kernel(scal, offs, old_ref, scale_ref, near_ref, far_ref, own_ref, other_ref, measured_ref, table_ref, *rest):
    outs, (keep_out, send_out, canvas_ref, probe_ref, grad, sums) = rest[:-6], rest[-6:]
    updated_canvas(scal, old_ref, scale_ref, (near_ref, far_ref), canvas_ref)
    place_probe(scal, own_ref, other_ref, probe_ref)
    terms_body(scal, offs, canvas_ref, probe_ref, measured_ref, table_ref, outs, keep_out, send_out, grad, sums)


def last_kernel(scal, own_ref, other_ref, probe_ref):
    place_probe(scal, own_ref, other_ref, probe_ref)


SMEM = pl.BlockSpec(memory_space=pltpu.SMEM)
VMEM = pl.BlockSpec(memory_space=pltpu.VMEM)
PARAMS = pltpu.CompilerParams(vmem_limit_bytes=32 * 1024 * 1024)


def f32(*shape):
    return jax.ShapeDtypeStruct(shape, jnp.float32)


def kernel_call(body, outs, operands, scratch=(), scalars=2, flops=0):
    return pl.pallas_call(
        body,
        out_shape=outs,
        in_specs=[SMEM] * scalars + [VMEM] * (len(operands) - scalars),
        out_specs=jax.tree.map(lambda _: VMEM, outs),
        scratch_shapes=[pltpu.VMEM(shape, jnp.float32) for shape in scratch],
        compiler_params=PARAMS,
        cost_estimate=pl.CostEstimate(flops=flops, bytes_accessed=1 << 20, transcendentals=0),
    )(*operands)


def fetch(tile, offs, halo):
    lanes = tile.shape[-1]
    odd_row, odd_col = (lax.axis_index(axis) % 2 == 1 for axis in ("sy", "sx"))
    upper, lower = tile[:, :halo].reshape(-1, lanes), tile[:, halo:].reshape(-1, lanes)
    near, far = jnp.where(odd_row, upper, lower), jnp.where(odd_row, lower, upper)
    own = jnp.pad((after(offs, near, far) + 1).astype(jnp.float32), ((0, 6), (0, lanes - offs.shape[1])))
    near, far = jnp.concatenate([near, own]), jnp.concatenate([far, own])
    rows_near, rows_far = swapped(near, "sy", False), partnered(swapped(far, "sy", True), "sy")
    side = after(tile, near, far)
    left = jnp.concatenate([side[0, :, :halo], side[1, :, :halo]], axis=1)
    right = jnp.concatenate([side[0, :, halo:], side[1, :, halo:]], axis=1)
    left, right = jnp.where(odd_col, left, right), jnp.where(odd_col, right, left)
    above, below = jnp.where(odd_row, rows_near, rows_far), jnp.where(odd_row, rows_far, rows_near)
    last = 2 * halo
    reach = jnp.concatenate([above[last : last + 2], own[:2], below[last : last + 2], own[6:]])

    def columns_of(middle, first):
        ends = []
        for rim in (above, below):
            rim = rim[:last].reshape(2, halo, lanes)
            half = [jnp.where(first, rim[part, :, :halo], rim[part, :, halo:]) for part in range(2)]
            ends.append(jnp.concatenate(half, axis=1))
        return jnp.concatenate([ends[0], middle, ends[1], reach])

    cols_near = swapped(columns_of(left, odd_col), "sx", False)
    cols_far = partnered(swapped(columns_of(right, ~odd_col), "sx", True), "sx")
    return rows_near, rows_far, cols_near, cols_far, reach


def corners_of(reaches, positions, extent):
    near, far, own = reaches[:8], reaches[8:16], reaches[16:]
    odd = lax.axis_index("sx") % 2 == 1
    sides = [jnp.where(odd, near, far), own, jnp.where(odd, far, near)]
    found = jnp.stack([side[:6, :positions].reshape(3, 2, positions) for side in sides], axis=1)
    found = found.reshape(9, 2, positions).astype(jnp.int32) - 1
    at = jnp.arange(9, dtype=jnp.int32)
    step = (jnp.stack([at // 3, at % 3], axis=1) - 1) * extent
    return jnp.where(found < 0, -extent, found + step[:, :, None])


def after(value, *others):
    return lax.optimization_barrier((value, *others))[0]


def chip_sum(both):
    return tree_sum([both[0]] + [flipped(both[t], "sy", 2 * t) for t in range(1, both.shape[0])])


def probe_fresh(parts, chunk):
    planes, rows, lanes = chunk.shape
    total = tree_sum(parts).reshape(planes + 1, rows, lanes)
    return chunk - PROBE_STEP * total[:planes] / (total[planes:] + REGULAR)


def across(total, start):
    return [total] + [flipped(total, "sx", t) for t in range(start, lax.axis_size("sx"))]


def probe_spread(fresh, chips):
    return jnp.stack([fresh] + [flipped(fresh, "sy", 2 * t) for t in range(1, chips)])


def per_device(object_tile, probe_modes, scan_offsets, intensities):
    tile = object_tile.shape[1]
    modes, _, extent, _ = probe_modes.shape
    halo = extent // 2
    size = tile + 2 * halo
    chips = lax.axis_size("sy") // 2
    rows = extent // 2 // chips
    planes = 2 * modes
    measured = intensities[0, 0]
    table = jnp.asarray(dft_tables(extent))
    scal = head_scalars(size, halo)
    offsets = scan_offsets[0, 0]
    positions = offsets.shape[0]
    offs = offsets.T
    kept = (chips, planes + 1, rows, extent)
    count = chips * (planes + 1) * rows
    rim_rows = 2 * 2 * halo
    quadrants = (f32(2, 2, tile, tile),) * 2
    rims = (f32(2, 2, tile, tile), f32(rim_rows, tile))
    scratch = ((2, 2, size, tile), (planes + 1, extent, extent))
    work = 2 * 3 * positions * 4 * (2 * extent) ** 3

    start = (lax.axis_index("sy") % 2 * chips + lax.axis_index("sy") // 2) * rows
    chunk = lax.dynamic_slice_in_dim(probe_modes.reshape(planes, extent, extent), start, rows, axis=1)
    halos = fetch(object_tile, offs, halo)

    def light(probe, corners):
        lit = (2, 2 * size, extent)
        return kernel_call(light_kernel, f32(2, size, tile), (scal, corners, probe), [lit], flops=work // 2)

    probe = probe_modes
    for iteration in range(ITERS):
        final = iteration == ITERS - 1
        sent = (count + rim_rows, extent) if final else kept
        outs = (rims if final else quadrants) + (f32(*kept), f32(*sent), f32(2, 2, size, tile))
        if iteration == 0:
            operands = (scal, offs, object_tile, *halos, probe, measured, table)
            outs = (f32(24, tile),) + outs
            reaches, *given, keep, send, canvas = kernel_call(first_kernel, outs, operands, scratch, flops=work)
        else:
            operands = (scal, offs, canvas, scale, near, far, own, other, measured, table)
            outs = outs + (f32(*probe.shape),)
            *given, keep, send, canvas, probe = kernel_call(next_kernel, outs, operands, scratch, flops=work)
        received = swapped(send, "sy", False)
        both = keep + received.reshape(-1, extent)[:count].reshape(kept)
        if iteration == 0:
            corners = corners_of(after(reaches, both), positions, tile)
        scale = light(probe, after(corners, both))
        if not final:
            side_a = given[0] + swapped(given[0], "sx", False)
            side_b = given[1] + partnered(swapped(given[1], "sx", True), "sx")
            near, far = jnp.stack([side_a[0], side_b[0]]), jnp.stack([side_a[1], side_b[1]])
            near = near + swapped(near, "sy", False)
            far = far + partnered(swapped(far, "sy", True), "sy")
            total = after(chip_sum(both), near, scale)
            chunk = after(probe_fresh(across(total, 1), chunk), near, far)
        else:
            own_rows, far = given
            far = swapped(far, "sy", True)
            total = after(chip_sum(both), far, scale).reshape(-1, extent)
            far = partnered(after(far, total), "sy")
            message = f32(total.shape[0] + tile, tile)
            middle, near, far = kernel_call(
                middle_kernel, (f32(2, tile, tile), message, message), (scal, own_rows, received, far, total), scalars=1
            )
            head = total.shape[0]
            near = flipped(near, "sx", 1)
            far = partnered(swapped(far[head:], "sx", True), "sx")
            parts = across(total, 2)
            parts.insert(1, near[:head])
            chunk = probe_fresh(parts, chunk)
            outcome = kernel_call(object_kernel, f32(2, tile, tile), (scal, canvas, scale, middle, near, far), scalars=1)
        own = probe_spread(chunk, chips)
        other = swapped(after(own, outcome) if final else own, "sy", False)
    return outcome, kernel_call(last_kernel, f32(*probe.shape), (scal, own, other), scalars=1)


def solution(mesh):
    placed = (P(None, "sy", "sx"), P(), P("sy", "sx", None, None), P("sy", "sx", None, None, None))
    return jax.shard_map(
        per_device,
        mesh=mesh,
        in_specs=placed,
        out_specs=(P(None, "sy", "sx"), P()),
        check_vma=False,
    )
```

```python
import functools

import jax
import jax.numpy as jnp
import numpy as np
from jax import lax
from jax.experimental import pallas as pl
from jax.experimental.pallas import tpu as pltpu
from jax.sharding import PartitionSpec as P

ITERS = 2
OBJECT_STEP = 0.5
PROBE_STEP = 2.0
REGULAR = 1.0


def dft_tables(extent):
    line = np.arange(extent)
    angle = (line[:, None] * line[None, :] % extent) * (2.0 * np.pi / extent)
    cosine, sine = np.cos(angle) / np.sqrt(extent), np.sin(angle) / np.sqrt(extent)
    table = np.block([[cosine, -sine], [sine, cosine]])
    high = table.astype(jnp.bfloat16)
    low = (table - high.astype(np.float64)).astype(jnp.bfloat16)
    return np.stack([high, low, high.T, low.T])


def split(values):
    high = values.astype(jnp.bfloat16)
    return high, (values - high.astype(jnp.float32)).astype(jnp.bfloat16)


def product(left, right):
    dot = functools.partial(jnp.dot, preferred_element_type=jnp.float32)
    return dot(left[0], right[0]) + (dot(left[0], right[1]) + dot(left[1], right[0]))


def swapped(values, axis, odd):
    if not odd:
        return lax.ppermute(values, axis, [(i, i ^ 1) for i in range(lax.axis_size(axis))])
    rows, cols = lax.axis_size("sy"), lax.axis_size("sx")
    pairs = []
    for row in range(rows):
        for col in range(cols):
            to_row, to_col = row, col
            if axis == "sy":
                to_row = (row + 1 if row % 2 else row - 1) % rows
            elif 0 < col < cols - 1:
                to_col = col + 1 if col % 2 else col - 1
            else:
                to_row = row ^ 1
            pairs.append((row * cols + col, to_row * cols + to_col))
    return lax.ppermute(values, ("sy", "sx"), pairs)


def partnered(received, axis):
    at = lax.axis_index(axis)
    return jnp.where((at == 0) | (at == lax.axis_size(axis) - 1), 0.0, received)


def flipped(values, axis, bits):
    return lax.ppermute(values, axis, [(i, i ^ bits) for i in range(lax.axis_size(axis))])


def tree_sum(parts):
    while len(parts) > 1:
        parts = [parts[i] + parts[i + 1] for i in range(0, len(parts), 2)]
    return parts[0]


def head_scalars(canvas_size, halo):
    row, col = lax.axis_index("sy"), lax.axis_index("sx")
    rows, cols = lax.axis_size("sy"), lax.axis_size("sx")
    head = [
        row % 2,
        col % 2,
        row // 2,
        jnp.where(row == 0, halo, 0),
        jnp.where(row == rows - 1, canvas_size - halo, canvas_size),
        jnp.where(col == 0, halo, 0),
        jnp.where(col == cols - 1, canvas_size - halo, canvas_size),
    ]
    return jnp.stack(head).astype(jnp.int32)


HEAD = 7


def light_kernel(scal, corners, probe_ref, scale_ref, lit):
    _, size, extent = scale_ref.shape
    lit[...] = jnp.zeros_like(lit)
    weight = sum(probe_ref[k, part] * probe_ref[k, part] for k in range(probe_ref.shape[0]) for part in range(2))
    lane = lax.broadcasted_iota(jnp.int32, (extent, extent), 1)

    for device in range(corners.shape[0]):
        for j in range(corners.shape[2]):
            row, col = corners[device, 0, j] + extent, corners[device, 1, j]
            moved = pltpu.roll(weight, col & (extent - 1), 1)
            for side in range(2):
                if device % 3 == 2 * (1 - side):
                    continue
                covered = (lane + side * extent >= col) & (lane + side * extent < col + extent)
                lit[side, pl.ds(row, extent), :] += jnp.where(covered, moved, 0.0)
    at_row = lax.broadcasted_iota(jnp.int32, (size, extent), 0)
    at_col = lax.broadcasted_iota(jnp.int32, (size, extent), 1)
    for side in range(2):
        inside = (at_row >= scal[3]) & (at_row < scal[4]) & (at_col + side * extent >= scal[5])
        inside = inside & (at_col + side * extent < scal[6])
        lighting = lit[side, extent : extent + size, :]
        scale_ref[side] = jnp.where(inside, OBJECT_STEP / (lighting + REGULAR), 0.0)


def updated_canvas(scal, old_ref, scale_ref, sums, canvas_ref):
    half = old_ref.shape[-1]
    for a in range(2):
        row = pl.multiple_of(jnp.where(scal[0] == a, half, 0), half)
        for b in range(2):
            side = jnp.where(scal[1] == b, 1, 0)
            scale = scale_ref[side, pl.ds(row, half)]
            for part in range(2):
                here = (part, side, pl.ds(row, half))
                canvas_ref[here] = old_ref[here] - scale * sums[a][b, part]


def place_probe(scal, own_ref, other_ref, probe_ref):
    chips, planes, rows, _ = own_ref.shape
    for slot in range(chips):
        chunk = scal[2] ^ slot
        for which, ref in ((scal[0], own_ref), (1 - scal[0], other_ref)):
            start = pl.multiple_of((which * chips + chunk) * rows, rows)
            for plane in range(planes):
                probe_ref[plane // 2, plane % 2, pl.ds(start, rows), :] = ref[slot, plane]


def terms_body(scal, offs, canvas_ref, probe_ref, measured_ref, table_ref, outs, keep_out, send_out, grad, sums):
    positions, extent, _ = measured_ref.shape
    modes = probe_ref.shape[0]
    w1 = (table_ref[0], table_ref[1])
    w2 = (table_ref[2], table_ref[3])
    grad[...] = jnp.zeros_like(grad)
    lane = lax.broadcasted_iota(jnp.int32, (extent, extent), 1)
    group = positions
    for first in range(0, positions, group):
        span = range(first, min(first + group, positions))
        patches = []
        for j in span:
            row, col = offs[0, j], offs[1, j]
            back = (extent - col) & (extent - 1)
            patches.append([
                jnp.where(
                    lane < extent - col,
                    pltpu.roll(canvas_ref[part, 0, pl.ds(row, extent), :], back, 1),
                    pltpu.roll(canvas_ref[part, 1, pl.ds(row, extent), :], back, 1),
                )
                for part in range(2)
            ])
        waves = []
        for o_r, o_i in patches:
            for k in range(modes):
                p_r, p_i = probe_ref[k, 0], probe_ref[k, 1]
                waves.append(jnp.concatenate([p_r * o_r - p_i * o_i, p_r * o_i + p_i * o_r], axis=1))
        count = len(waves)
        half = product(split(jnp.concatenate(waves, axis=0)), w1)
        rows = [half[k * extent : (k + 1) * extent] for k in range(count)]
        half = jnp.concatenate(
            [jnp.concatenate([r[:, part * extent : (part + 1) * extent] for r in rows], axis=1) for part in range(2)],
            axis=0,
        )
        spectrum = product(w2, split(half))
        squares = spectrum * spectrum
        power = squares[:extent] + squares[extent:]
        wide = []
        for at, j in enumerate(span):
            misfit = sum(power[:, k * extent : (k + 1) * extent] for k in range(at * modes, (at + 1) * modes)) - measured_ref[j]
            wide += [misfit] * modes
        wide = jnp.concatenate(wide, axis=1)
        weighted = spectrum * jnp.concatenate([wide, wide], axis=0)
        half = product(w1, split(weighted))
        half = jnp.concatenate(
            [
                jnp.concatenate([half[:extent, k * extent : (k + 1) * extent], half[extent:, k * extent : (k + 1) * extent]], axis=1)
                for k in range(count)
            ],
            axis=0,
        )
        chi = product(split(half), w2)
        for at, j in enumerate(span):
            o_r, o_i = patches[at]
            row, col = offs[0, j], offs[1, j]
            turn = col & (extent - 1)
            g_r = g_i = 0.0
            for k in range(modes):
                p_r, p_i = probe_ref[k, 0], probe_ref[k, 1]
                wave = at * modes + k
                c_r = chi[wave * extent : (wave + 1) * extent, :extent]
                c_i = chi[wave * extent : (wave + 1) * extent, extent:]
                g_r = g_r + (p_r * c_r + p_i * c_i)
                g_i = g_i + (p_r * c_i - p_i * c_r)
                for part, term in ((0, o_r * c_r + o_i * c_i), (1, o_r * c_i - o_i * c_r)):
                    plane = 2 * k + part
                    sums[plane] = term if j == 0 else sums[plane] + term
            term = o_r * o_r + o_i * o_i
            sums[2 * modes] = term if j == 0 else sums[2 * modes] + term
            for plane, term in enumerate((g_r, g_i)):
                moved = pltpu.roll(term, turn, 1)
                grad[plane, 0, pl.ds(row, extent), :] += jnp.where(lane >= col, moved, 0.0)
                grad[plane, 1, pl.ds(row, extent), :] += jnp.where(lane < col, moved, 0.0)
    if len(outs[0].shape) == len(outs[1].shape):
        give_quadrants(scal, grad, outs)
    else:
        give_rims(scal, grad, outs, send_out)
    chips, planes, rows, _ = keep_out.shape
    for slot in range(chips):
        chunk = scal[2] ^ slot
        for which, ref in ((scal[0], keep_out), (1 - scal[0], send_out)):
            start = pl.multiple_of((which * chips + chunk) * rows, rows)
            for plane in range(planes):
                piece = sums[plane, pl.ds(start, rows), :]
                if len(ref.shape) == 2:
                    at = (slot * planes + plane) * rows
                    ref[at : at + rows, :] = piece
                else:
                    ref[slot, plane] = piece


def give_quadrants(scal, grad, outs):
    extent = grad.shape[-1]
    for a in range(2):
        row = pl.multiple_of(jnp.where(scal[0] == a, extent, 0), extent)
        for b in range(2):
            side = jnp.where(scal[1] == b, 1, 0)
            for plane in range(grad.shape[0]):
                outs[b][a, plane] = grad[plane, side, pl.ds(row, extent), :]


def give_rims(scal, grad, outs, send_out):
    planes, sides, size, extent = grad.shape
    halo = extent // 2
    base = send_out.shape[0] - planes * sides * halo
    outer = (pl.multiple_of(jnp.where(scal[0] == 1, 0, size - halo), halo), pl.multiple_of(jnp.where(scal[0] == 1, size - halo, 0), halo))
    for plane in range(planes):
        for side in range(sides):
            at = (plane * sides + side) * halo
            outs[0][plane, side] = grad[plane, side, halo : size - halo, :]
            send_out[base + at : base + at + halo, :] = grad[plane, side, pl.ds(outer[0], halo), :]
            outs[1][at : at + halo, :] = grad[plane, side, pl.ds(outer[1], halo), :]


def middle_kernel(scal, own_ref, near_ref, far_ref, middle_ref, near_out, far_out):
    planes, sides, extent, _ = own_ref.shape
    halo = extent // 2
    base = near_ref.shape[0] - planes * sides * halo
    odd_row, odd_col = scal[0] == 1, scal[1] == 1
    lane = lax.broadcasted_iota(jnp.int32, (extent, extent), 1)
    rims = []
    for plane in range(planes):
        rows = []
        for side in range(sides):
            at = (plane * sides + side) * halo
            near, far = near_ref[base + at : base + at + halo, :], far_ref[at : at + halo, :]
            other = jnp.concatenate([jnp.where(odd_row, near, far), jnp.where(odd_row, far, near)], axis=0)
            rows.append(own_ref[plane, side] + other)
        turned = [pltpu.roll(part, halo, 1) for part in rows]
        middle_ref[plane] = jnp.where(lane < halo, turned[0], turned[1])
        rims.append((rows[0], turned[1]) if plane == 0 else (turned[0], rows[1]))
    left, right = (jnp.where(lane < halo, rims[0][side], rims[1][side]) for side in range(sides))
    near_out[...] = jnp.where(odd_col, left, right)
    far_out[...] = jnp.where(odd_col, right, left)


def object_kernel(scal, old_ref, scale_ref, middle_ref, near_ref, far_ref, object_ref):
    extent = old_ref.shape[-1]
    halo = extent // 2
    lane = lax.broadcasted_iota(jnp.int32, (extent, extent), 1)
    middle = pl.ds(halo, extent)

    def tile_of(sides):
        return jnp.where(lane < halo, pltpu.roll(sides[0], halo, 1), pltpu.roll(sides[1], halo, 1))

    scale = tile_of([scale_ref[side, middle] for side in range(2)])
    odd = scal[1] == 1
    near, far = near_ref[...], far_ref[...]
    left = jnp.where(scal[5] > 0, 0.0, jnp.where(odd, near, far))
    right = jnp.where(scal[6] < 2 * extent, 0.0, jnp.where(odd, far, near))
    for part in range(2):
        if part == 0:
            beside = jnp.where(lane < halo, left, pltpu.roll(right, halo, 1))
        else:
            beside = jnp.where(lane < halo, pltpu.roll(left, halo, 1), right)
        old = tile_of([old_ref[part, side, middle] for side in range(2)])
        object_ref[part] = old - scale * (middle_ref[part] + beside)


def first_kernel(
    scal, offs, tile_ref, rows_near, rows_far, cols_near, cols_far, reach, probe_ref, measured_ref, table_ref,
    reaches_out, *rest,
):
    reaches_out[0:8, :], reaches_out[8:16, :], reaches_out[16:24, :] = cols_near[-8:, :], cols_far[-8:, :], reach[...]
    outs, (keep_out, send_out, canvas_ref, grad, sums) = rest[:-5], rest[-5:]
    extent = tile_ref.shape[-1]
    halo = extent // 2
    size = 2 * extent
    odd_row, odd_col = scal[0] == 1, scal[1] == 1
    lane = lax.broadcasted_iota(jnp.int32, (extent, extent), 1)
    for part in range(2):
        near, far = (ref[part * halo : (part + 1) * halo] for ref in (rows_near, rows_far))
        above, below = jnp.where(odd_row, near, far), jnp.where(odd_row, far, near)
        for start in range(0, size, extent):
            half = pl.ds(start, extent)
            if start == 0:
                middle = jnp.concatenate([above, tile_ref[part, :halo]], axis=0)
            else:
                middle = jnp.concatenate([tile_ref[part, halo:], below], axis=0)
            middle = pltpu.roll(middle, halo, 1)
            near, far = cols_near[half], cols_far[half]
            if part == 1:
                near, far = pltpu.roll(near, halo, 1), pltpu.roll(far, halo, 1)
            left, right = jnp.where(odd_col, near, far), jnp.where(odd_col, far, near)
            canvas_ref[part, 0, half] = jnp.where(lane < halo, left, middle)
            canvas_ref[part, 1, half] = jnp.where(lane < halo, middle, pltpu.roll(right, halo, 1))
    terms_body(scal, offs, canvas_ref, probe_ref, measured_ref, table_ref, outs, keep_out, send_out, grad, sums)


def next_kernel(scal, offs, old_ref, scale_ref, near_ref, far_ref, own_ref, other_ref, measured_ref, table_ref, *rest):
    outs, (keep_out, send_out, canvas_ref, probe_ref, grad, sums) = rest[:-6], rest[-6:]
    updated_canvas(scal, old_ref, scale_ref, (near_ref, far_ref), canvas_ref)
    place_probe(scal, own_ref, other_ref, probe_ref)
    terms_body(scal, offs, canvas_ref, probe_ref, measured_ref, table_ref, outs, keep_out, send_out, grad, sums)


def last_kernel(scal, own_ref, other_ref, probe_ref):
    place_probe(scal, own_ref, other_ref, probe_ref)


SMEM = pl.BlockSpec(memory_space=pltpu.SMEM)
VMEM = pl.BlockSpec(memory_space=pltpu.VMEM)
PARAMS = pltpu.CompilerParams(vmem_limit_bytes=32 * 1024 * 1024)


def f32(*shape):
    return jax.ShapeDtypeStruct(shape, jnp.float32)


def kernel_call(body, outs, operands, scratch=(), scalars=2, flops=0):
    return pl.pallas_call(
        body,
        out_shape=outs,
        in_specs=[SMEM] * scalars + [VMEM] * (len(operands) - scalars),
        out_specs=jax.tree.map(lambda _: VMEM, outs),
        scratch_shapes=[pltpu.VMEM(shape, jnp.float32) for shape in scratch],
        compiler_params=PARAMS,
        cost_estimate=pl.CostEstimate(flops=flops, bytes_accessed=1 << 20, transcendentals=0),
    )(*operands)


def fetch(tile, offs, halo):
    lanes = tile.shape[-1]
    odd_row, odd_col = (lax.axis_index(axis) % 2 == 1 for axis in ("sy", "sx"))
    upper, lower = tile[:, :halo].reshape(-1, lanes), tile[:, halo:].reshape(-1, lanes)
    near, far = jnp.where(odd_row, upper, lower), jnp.where(odd_row, lower, upper)
    own = jnp.pad((after(offs, near, far) + 1).astype(jnp.float32), ((0, 6), (0, lanes - offs.shape[1])))
    near, far = jnp.concatenate([near, own]), jnp.concatenate([far, own])
    rows_near, rows_far = swapped(near, "sy", False), partnered(swapped(far, "sy", True), "sy")
    side = after(tile, near, far)
    left = jnp.concatenate([side[0, :, :halo], side[1, :, :halo]], axis=1)
    right = jnp.concatenate([side[0, :, halo:], side[1, :, halo:]], axis=1)
    left, right = jnp.where(odd_col, left, right), jnp.where(odd_col, right, left)
    above, below = jnp.where(odd_row, rows_near, rows_far), jnp.where(odd_row, rows_far, rows_near)
    last = 2 * halo
    reach = jnp.concatenate([above[last : last + 2], own[:2], below[last : last + 2], own[6:]])

    def columns_of(middle, first):
        ends = []
        for rim in (above, below):
            rim = rim[:last].reshape(2, halo, lanes)
            half = [jnp.where(first, rim[part, :, :halo], rim[part, :, halo:]) for part in range(2)]
            ends.append(jnp.concatenate(half, axis=1))
        return jnp.concatenate([ends[0], middle, ends[1], reach])

    cols_near = swapped(columns_of(left, odd_col), "sx", False)
    cols_far = partnered(swapped(columns_of(right, ~odd_col), "sx", True), "sx")
    return rows_near, rows_far, cols_near, cols_far, reach


def corners_of(reaches, positions, extent):
    near, far, own = reaches[:8], reaches[8:16], reaches[16:]
    odd = lax.axis_index("sx") % 2 == 1
    sides = [jnp.where(odd, near, far), own, jnp.where(odd, far, near)]
    found = jnp.stack([side[:6, :positions].reshape(3, 2, positions) for side in sides], axis=1)
    found = found.reshape(9, 2, positions).astype(jnp.int32) - 1
    at = jnp.arange(9, dtype=jnp.int32)
    step = (jnp.stack([at // 3, at % 3], axis=1) - 1) * extent
    return jnp.where(found < 0, -extent, found + step[:, :, None])


def after(value, *others):
    return lax.optimization_barrier((value, *others))[0]


def chip_sum(both):
    return tree_sum([both[0]] + [flipped(both[t], "sy", 2 * t) for t in range(1, both.shape[0])])


def probe_fresh(parts, chunk):
    planes, rows, lanes = chunk.shape
    total = tree_sum(parts).reshape(planes + 1, rows, lanes)
    return chunk - PROBE_STEP * total[:planes] / (total[planes:] + REGULAR)


def across(total, start):
    return [total] + [flipped(total, "sx", t) for t in range(start, lax.axis_size("sx"))]


def probe_spread(fresh, chips):
    return jnp.stack([fresh] + [flipped(fresh, "sy", 2 * t) for t in range(1, chips)])


def per_device(object_tile, probe_modes, scan_offsets, intensities):
    tile = object_tile.shape[1]
    modes, _, extent, _ = probe_modes.shape
    halo = extent // 2
    size = tile + 2 * halo
    chips = lax.axis_size("sy") // 2
    rows = extent // 2 // chips
    planes = 2 * modes
    measured = intensities[0, 0]
    table = jnp.asarray(dft_tables(extent))
    scal = head_scalars(size, halo)
    offsets = scan_offsets[0, 0]
    positions = offsets.shape[0]
    offs = offsets.T
    kept = (chips, planes + 1, rows, extent)
    count = chips * (planes + 1) * rows
    rim_rows = 2 * 2 * halo
    quadrants = (f32(2, 2, tile, tile),) * 2
    rims = (f32(2, 2, tile, tile), f32(rim_rows, tile))
    scratch = ((2, 2, size, tile), (planes + 1, extent, extent))
    work = 2 * 3 * positions * 4 * (2 * extent) ** 3

    start = (lax.axis_index("sy") % 2 * chips + lax.axis_index("sy") // 2) * rows
    chunk = lax.dynamic_slice_in_dim(probe_modes.reshape(planes, extent, extent), start, rows, axis=1)
    halos = fetch(object_tile, offs, halo)

    def light(probe, corners):
        lit = (2, 2 * size, extent)
        return kernel_call(light_kernel, f32(2, size, tile), (scal, corners, probe), [lit], flops=work // 2)

    probe = probe_modes
    for iteration in range(ITERS):
        final = iteration == ITERS - 1
        sent = (count + rim_rows, extent) if final else kept
        outs = (rims if final else quadrants) + (f32(*kept), f32(*sent), f32(2, 2, size, tile))
        if iteration == 0:
            operands = (scal, offs, object_tile, *halos, probe, measured, table)
            outs = (f32(24, tile),) + outs
            reaches, *given, keep, send, canvas = kernel_call(first_kernel, outs, operands, scratch, flops=work)
        else:
            operands = (scal, offs, canvas, scale, near, far, own, other, measured, table)
            outs = outs + (f32(*probe.shape),)
            *given, keep, send, canvas, probe = kernel_call(next_kernel, outs, operands, scratch, flops=work)
        received = swapped(send, "sy", False)
        both = keep + received.reshape(-1, extent)[:count].reshape(kept)
        if iteration == 0:
            corners = corners_of(after(reaches, both), positions, tile)
        scale = light(probe, after(corners, both))
        if not final:
            side_b = given[1] + partnered(swapped(given[1], "sx", True), "sx")
            side_a = given[0] + swapped(given[0], "sx", False)
            near, far = jnp.stack([side_a[0], side_b[0]]), jnp.stack([side_a[1], side_b[1]])
            near = near + swapped(near, "sy", False)
            far = far + partnered(swapped(far, "sy", True), "sy")
            total = after(chip_sum(both), near, scale)
            chunk = after(probe_fresh(across(total, 1), chunk), near, far)
        else:
            own_rows, far = given
            far = swapped(far, "sy", True)
            total = after(chip_sum(both), far, scale)
            far = partnered(after(far, total), "sy")
            middle, near, far = kernel_call(
                middle_kernel, (f32(2, tile, tile),) + (f32(tile, tile),) * 2, (scal, own_rows, received, far), scalars=1
            )
            near = swapped(near, "sx", False)
            far = partnered(swapped(far, "sx", True), "sx")
            parts = across(total, 1)
            chunk = probe_fresh(parts, chunk)
            outcome = kernel_call(object_kernel, f32(2, tile, tile), (scal, canvas, scale, middle, near, far), scalars=1)
        own = probe_spread(chunk, chips)
        other = swapped(after(own, outcome) if final else own, "sy", False)
    return outcome, kernel_call(last_kernel, f32(*probe.shape), (scal, own, other), scalars=1)


def solution(mesh):
    placed = (P(None, "sy", "sx"), P(), P("sy", "sx", None, None), P("sy", "sx", None, None, None))
    return jax.shard_map(
        per_device,
        mesh=mesh,
        in_specs=placed,
        out_specs=(P(None, "sy", "sx"), P()),
        check_vma=False,
    )
```

```python
import functools

import jax
import jax.numpy as jnp
import numpy as np
from jax import lax
from jax.experimental import pallas as pl
from jax.experimental.pallas import tpu as pltpu
from jax.sharding import PartitionSpec as P

ITERS = 2
OBJECT_STEP = 0.5
PROBE_STEP = 2.0
REGULAR = 1.0


def dft_tables(extent):
    line = np.arange(extent)
    angle = (line[:, None] * line[None, :] % extent) * (2.0 * np.pi / extent)
    cosine, sine = np.cos(angle) / np.sqrt(extent), np.sin(angle) / np.sqrt(extent)
    table = np.block([[cosine, -sine], [sine, cosine]])
    high = table.astype(jnp.bfloat16)
    low = (table - high.astype(np.float64)).astype(jnp.bfloat16)
    return np.stack([high, low, high.T, low.T])


def split(values):
    high = values.astype(jnp.bfloat16)
    return high, (values - high.astype(jnp.float32)).astype(jnp.bfloat16)


def product(left, right):
    dot = functools.partial(jnp.dot, preferred_element_type=jnp.float32)
    return dot(left[0], right[0]) + (dot(left[0], right[1]) + dot(left[1], right[0]))


def swapped(values, axis, odd):
    if not odd:
        return lax.ppermute(values, axis, [(i, i ^ 1) for i in range(lax.axis_size(axis))])
    rows, cols = lax.axis_size("sy"), lax.axis_size("sx")
    pairs = []
    for row in range(rows):
        for col in range(cols):
            to_row, to_col = row, col
            if axis == "sy":
                if 0 < row < rows - 1:
                    to_row = row + 1 if row % 2 else row - 1
                else:
                    to_col = col ^ 1
            elif 0 < col < cols - 1:
                to_col = col + 1 if col % 2 else col - 1
            else:
                to_row = row ^ 1
            pairs.append((row * cols + col, to_row * cols + to_col))
    return lax.ppermute(values, ("sy", "sx"), pairs)


def partnered(received, axis):
    at = lax.axis_index(axis)
    return jnp.where((at == 0) | (at == lax.axis_size(axis) - 1), 0.0, received)


def flipped(values, axis, bits):
    return lax.ppermute(values, axis, [(i, i ^ bits) for i in range(lax.axis_size(axis))])


def tree_sum(parts):
    while len(parts) > 1:
        parts = [parts[i] + parts[i + 1] for i in range(0, len(parts), 2)]
    return parts[0]


def head_scalars(canvas_size, halo):
    row, col = lax.axis_index("sy"), lax.axis_index("sx")
    rows, cols = lax.axis_size("sy"), lax.axis_size("sx")
    head = [
        row % 2,
        col % 2,
        row // 2,
        jnp.where(row == 0, halo, 0),
        jnp.where(row == rows - 1, canvas_size - halo, canvas_size),
        jnp.where(col == 0, halo, 0),
        jnp.where(col == cols - 1, canvas_size - halo, canvas_size),
    ]
    return jnp.stack(head).astype(jnp.int32)


HEAD = 7


def light_kernel(scal, corners, probe_ref, scale_ref, lit):
    _, size, extent = scale_ref.shape
    lit[...] = jnp.zeros_like(lit)
    weight = sum(probe_ref[k, part] * probe_ref[k, part] for k in range(probe_ref.shape[0]) for part in range(2))
    lane = lax.broadcasted_iota(jnp.int32, (extent, extent), 1)

    for device in range(corners.shape[0]):
        for j in range(corners.shape[2]):
            row, col = corners[device, 0, j] + extent, corners[device, 1, j]
            moved = pltpu.roll(weight, col & (extent - 1), 1)
            for side in range(2):
                if device % 3 == 2 * (1 - side):
                    continue
                covered = (lane + side * extent >= col) & (lane + side * extent < col + extent)
                lit[side, pl.ds(row, extent), :] += jnp.where(covered, moved, 0.0)
    at_row = lax.broadcasted_iota(jnp.int32, (size, extent), 0)
    at_col = lax.broadcasted_iota(jnp.int32, (size, extent), 1)
    for side in range(2):
        inside = (at_row >= scal[3]) & (at_row < scal[4]) & (at_col + side * extent >= scal[5])
        inside = inside & (at_col + side * extent < scal[6])
        lighting = lit[side, extent : extent + size, :]
        scale_ref[side] = jnp.where(inside, OBJECT_STEP / (lighting + REGULAR), 0.0)


def updated_canvas(scal, old_ref, scale_ref, sums, canvas_ref):
    half = old_ref.shape[-1]
    for a in range(2):
        row = pl.multiple_of(jnp.where(scal[0] == a, half, 0), half)
        for b in range(2):
            side = jnp.where(scal[1] == b, 1, 0)
            scale = scale_ref[side, pl.ds(row, half)]
            for part in range(2):
                here = (part, side, pl.ds(row, half))
                canvas_ref[here] = old_ref[here] - scale * sums[a][b, part]


def place_probe(scal, own_ref, other_ref, probe_ref):
    chips, planes, rows, _ = own_ref.shape
    for slot in range(chips):
        chunk = scal[2] ^ slot
        for which, ref in ((scal[0], own_ref), (1 - scal[0], other_ref)):
            start = pl.multiple_of((which * chips + chunk) * rows, rows)
            for plane in range(planes):
                probe_ref[plane // 2, plane % 2, pl.ds(start, rows), :] = ref[slot, plane]


def terms_body(scal, offs, canvas_ref, probe_ref, measured_ref, table_ref, outs, keep_out, send_out, grad, sums):
    positions, extent, _ = measured_ref.shape
    modes = probe_ref.shape[0]
    w1 = (table_ref[0], table_ref[1])
    w2 = (table_ref[2], table_ref[3])
    grad[...] = jnp.zeros_like(grad)
    lane = lax.broadcasted_iota(jnp.int32, (extent, extent), 1)
    group = positions
    for first in range(0, positions, group):
        span = range(first, min(first + group, positions))
        patches = []
        for j in span:
            row, col = offs[0, j], offs[1, j]
            back = (extent - col) & (extent - 1)
            patches.append([
                jnp.where(
                    lane < extent - col,
                    pltpu.roll(canvas_ref[part, 0, pl.ds(row, extent), :], back, 1),
                    pltpu.roll(canvas_ref[part, 1, pl.ds(row, extent), :], back, 1),
                )
                for part in range(2)
            ])
        waves = []
        for o_r, o_i in patches:
            for k in range(modes):
                p_r, p_i = probe_ref[k, 0], probe_ref[k, 1]
                waves.append(jnp.concatenate([p_r * o_r - p_i * o_i, p_r * o_i + p_i * o_r], axis=1))
        count = len(waves)
        half = product(split(jnp.concatenate(waves, axis=0)), w1)
        rows = [half[k * extent : (k + 1) * extent] for k in range(count)]
        half = jnp.concatenate(
            [jnp.concatenate([r[:, part * extent : (part + 1) * extent] for r in rows], axis=1) for part in range(2)],
            axis=0,
        )
        spectrum = product(w2, split(half))
        squares = spectrum * spectrum
        power = squares[:extent] + squares[extent:]
        wide = []
        for at, j in enumerate(span):
            misfit = sum(power[:, k * extent : (k + 1) * extent] for k in range(at * modes, (at + 1) * modes)) - measured_ref[j]
            wide += [misfit] * modes
        wide = jnp.concatenate(wide, axis=1)
        weighted = spectrum * jnp.concatenate([wide, wide], axis=0)
        half = product(w1, split(weighted))
        half = jnp.concatenate(
            [
                jnp.concatenate([half[:extent, k * extent : (k + 1) * extent], half[extent:, k * extent : (k + 1) * extent]], axis=1)
                for k in range(count)
            ],
            axis=0,
        )
        chi = product(split(half), w2)
        for at, j in enumerate(span):
            o_r, o_i = patches[at]
            row, col = offs[0, j], offs[1, j]
            turn = col & (extent - 1)
            g_r = g_i = 0.0
            for k in range(modes):
                p_r, p_i = probe_ref[k, 0], probe_ref[k, 1]
                wave = at * modes + k
                c_r = chi[wave * extent : (wave + 1) * extent, :extent]
                c_i = chi[wave * extent : (wave + 1) * extent, extent:]
                g_r = g_r + (p_r * c_r + p_i * c_i)
                g_i = g_i + (p_r * c_i - p_i * c_r)
                for part, term in ((0, o_r * c_r + o_i * c_i), (1, o_r * c_i - o_i * c_r)):
                    plane = 2 * k + part
                    sums[plane] = term if j == 0 else sums[plane] + term
            term = o_r * o_r + o_i * o_i
            sums[2 * modes] = term if j == 0 else sums[2 * modes] + term
            for plane, term in enumerate((g_r, g_i)):
                moved = pltpu.roll(term, turn, 1)
                grad[plane, 0, pl.ds(row, extent), :] += jnp.where(lane >= col, moved, 0.0)
                grad[plane, 1, pl.ds(row, extent), :] += jnp.where(lane < col, moved, 0.0)
    if len(outs[0].shape) == len(outs[1].shape):
        give_quadrants(scal, grad, outs)
    else:
        give_rims(scal, grad, outs, send_out)
    chips, planes, rows, _ = keep_out.shape
    for slot in range(chips):
        chunk = scal[2] ^ slot
        for which, ref in ((scal[0], keep_out), (1 - scal[0], send_out)):
            start = pl.multiple_of((which * chips + chunk) * rows, rows)
            for plane in range(planes):
                piece = sums[plane, pl.ds(start, rows), :]
                if len(ref.shape) == 2:
                    at = (slot * planes + plane) * rows
                    ref[at : at + rows, :] = piece
                else:
                    ref[slot, plane] = piece


def give_quadrants(scal, grad, outs):
    extent = grad.shape[-1]
    for a in range(2):
        row = pl.multiple_of(jnp.where(scal[0] == a, extent, 0), extent)
        for b in range(2):
            side = jnp.where(scal[1] == b, 1, 0)
            for plane in range(grad.shape[0]):
                outs[b][a, plane] = grad[plane, side, pl.ds(row, extent), :]


def give_rims(scal, grad, outs, send_out):
    planes, sides, size, extent = grad.shape
    halo = extent // 2
    base = send_out.shape[0] - planes * sides * halo
    outer = (pl.multiple_of(jnp.where(scal[0] == 1, 0, size - halo), halo), pl.multiple_of(jnp.where(scal[0] == 1, size - halo, 0), halo))
    for plane in range(planes):
        for side in range(sides):
            at = (plane * sides + side) * halo
            outs[0][plane, side] = grad[plane, side, halo : size - halo, :]
            send_out[base + at : base + at + halo, :] = grad[plane, side, pl.ds(outer[0], halo), :]
            outs[1][at : at + halo, :] = grad[plane, side, pl.ds(outer[1], halo), :]


def middle_kernel(scal, own_ref, near_ref, far_ref, middle_ref, near_out, far_out):
    planes, sides, extent, _ = own_ref.shape
    halo = extent // 2
    base = near_ref.shape[0] - planes * sides * halo
    odd_row, odd_col = scal[0] == 1, scal[1] == 1
    lane = lax.broadcasted_iota(jnp.int32, (extent, extent), 1)
    rims = []
    for plane in range(planes):
        rows = []
        for side in range(sides):
            at = (plane * sides + side) * halo
            near, far = near_ref[base + at : base + at + halo, :], far_ref[at : at + halo, :]
            other = jnp.concatenate([jnp.where(odd_row, near, far), jnp.where(odd_row, far, near)], axis=0)
            rows.append(own_ref[plane, side] + other)
        turned = [pltpu.roll(part, halo, 1) for part in rows]
        middle_ref[plane] = jnp.where(lane < halo, turned[0], turned[1])
        rims.append((rows[0], turned[1]) if plane == 0 else (turned[0], rows[1]))
    left, right = (jnp.where(lane < halo, rims[0][side], rims[1][side]) for side in range(sides))
    near_out[...] = jnp.where(odd_col, left, right)
    far_out[...] = jnp.where(odd_col, right, left)


def object_kernel(scal, old_ref, scale_ref, middle_ref, near_ref, far_ref, object_ref):
    extent = old_ref.shape[-1]
    halo = extent // 2
    lane = lax.broadcasted_iota(jnp.int32, (extent, extent), 1)
    middle = pl.ds(halo, extent)

    def tile_of(sides):
        return jnp.where(lane < halo, pltpu.roll(sides[0], halo, 1), pltpu.roll(sides[1], halo, 1))

    scale = tile_of([scale_ref[side, middle] for side in range(2)])
    odd = scal[1] == 1
    near, far = near_ref[...], far_ref[...]
    left = jnp.where(scal[5] > 0, 0.0, jnp.where(odd, near, far))
    right = jnp.where(scal[6] < 2 * extent, 0.0, jnp.where(odd, far, near))
    for part in range(2):
        if part == 0:
            beside = jnp.where(lane < halo, left, pltpu.roll(right, halo, 1))
        else:
            beside = jnp.where(lane < halo, pltpu.roll(left, halo, 1), right)
        old = tile_of([old_ref[part, side, middle] for side in range(2)])
        object_ref[part] = old - scale * (middle_ref[part] + beside)


def first_kernel(
    scal, offs, tile_ref, rows_near, rows_far, cols_near, cols_far, reach, probe_ref, measured_ref, table_ref,
    reaches_out, *rest,
):
    reaches_out[0:8, :], reaches_out[8:16, :], reaches_out[16:24, :] = cols_near[-8:, :], cols_far[-8:, :], reach[...]
    outs, (keep_out, send_out, canvas_ref, grad, sums) = rest[:-5], rest[-5:]
    extent = tile_ref.shape[-1]
    halo = extent // 2
    size = 2 * extent
    odd_row, odd_col = scal[0] == 1, scal[1] == 1
    lane = lax.broadcasted_iota(jnp.int32, (extent, extent), 1)
    for part in range(2):
        near, far = (ref[part * halo : (part + 1) * halo] for ref in (rows_near, rows_far))
        above, below = jnp.where(odd_row, near, far), jnp.where(odd_row, far, near)
        for start in range(0, size, extent):
            half = pl.ds(start, extent)
            if start == 0:
                middle = jnp.concatenate([above, tile_ref[part, :halo]], axis=0)
            else:
                middle = jnp.concatenate([tile_ref[part, halo:], below], axis=0)
            middle = pltpu.roll(middle, halo, 1)
            near, far = cols_near[half], cols_far[half]
            if part == 1:
                near, far = pltpu.roll(near, halo, 1), pltpu.roll(far, halo, 1)
            left, right = jnp.where(odd_col, near, far), jnp.where(odd_col, far, near)
            canvas_ref[part, 0, half] = jnp.where(lane < halo, left, middle)
            canvas_ref[part, 1, half] = jnp.where(lane < halo, middle, pltpu.roll(right, halo, 1))
    terms_body(scal, offs, canvas_ref, probe_ref, measured_ref, table_ref, outs, keep_out, send_out, grad, sums)


def next_kernel(scal, offs, old_ref, scale_ref, near_ref, far_ref, own_ref, other_ref, measured_ref, table_ref, *rest):
    outs, (keep_out, send_out, canvas_ref, probe_ref, grad, sums) = rest[:-6], rest[-6:]
    updated_canvas(scal, old_ref, scale_ref, (near_ref, far_ref), canvas_ref)
    place_probe(scal, own_ref, other_ref, probe_ref)
    terms_body(scal, offs, canvas_ref, probe_ref, measured_ref, table_ref, outs, keep_out, send_out, grad, sums)


def last_kernel(scal, own_ref, other_ref, probe_ref):
    place_probe(scal, own_ref, other_ref, probe_ref)


SMEM = pl.BlockSpec(memory_space=pltpu.SMEM)
VMEM = pl.BlockSpec(memory_space=pltpu.VMEM)
PARAMS = pltpu.CompilerParams(vmem_limit_bytes=32 * 1024 * 1024)


def f32(*shape):
    return jax.ShapeDtypeStruct(shape, jnp.float32)


def kernel_call(body, outs, operands, scratch=(), scalars=2, flops=0):
    return pl.pallas_call(
        body,
        out_shape=outs,
        in_specs=[SMEM] * scalars + [VMEM] * (len(operands) - scalars),
        out_specs=jax.tree.map(lambda _: VMEM, outs),
        scratch_shapes=[pltpu.VMEM(shape, jnp.float32) for shape in scratch],
        compiler_params=PARAMS,
        cost_estimate=pl.CostEstimate(flops=flops, bytes_accessed=1 << 20, transcendentals=0),
    )(*operands)


def fetch(tile, offs, halo):
    lanes = tile.shape[-1]
    odd_row, odd_col = (lax.axis_index(axis) % 2 == 1 for axis in ("sy", "sx"))
    upper, lower = tile[:, :halo].reshape(-1, lanes), tile[:, halo:].reshape(-1, lanes)
    near, far = jnp.where(odd_row, upper, lower), jnp.where(odd_row, lower, upper)
    own = jnp.pad((after(offs, near, far) + 1).astype(jnp.float32), ((0, 6), (0, lanes - offs.shape[1])))
    near, far = jnp.concatenate([near, own]), jnp.concatenate([far, own])
    rows_near, rows_far = swapped(near, "sy", False), partnered(swapped(far, "sy", True), "sy")
    side = after(tile, near, far)
    left = jnp.concatenate([side[0, :, :halo], side[1, :, :halo]], axis=1)
    right = jnp.concatenate([side[0, :, halo:], side[1, :, halo:]], axis=1)
    left, right = jnp.where(odd_col, left, right), jnp.where(odd_col, right, left)
    above, below = jnp.where(odd_row, rows_near, rows_far), jnp.where(odd_row, rows_far, rows_near)
    last = 2 * halo
    reach = jnp.concatenate([above[last : last + 2], own[:2], below[last : last + 2], own[6:]])

    def columns_of(middle, first):
        ends = []
        for rim in (above, below):
            rim = rim[:last].reshape(2, halo, lanes)
            half = [jnp.where(first, rim[part, :, :halo], rim[part, :, halo:]) for part in range(2)]
            ends.append(jnp.concatenate(half, axis=1))
        return jnp.concatenate([ends[0], middle, ends[1], reach])

    cols_near = swapped(columns_of(left, odd_col), "sx", False)
    cols_far = partnered(swapped(columns_of(right, ~odd_col), "sx", True), "sx")
    return rows_near, rows_far, cols_near, cols_far, reach


def corners_of(reaches, positions, extent):
    near, far, own = reaches[:8], reaches[8:16], reaches[16:]
    odd = lax.axis_index("sx") % 2 == 1
    sides = [jnp.where(odd, near, far), own, jnp.where(odd, far, near)]
    found = jnp.stack([side[:6, :positions].reshape(3, 2, positions) for side in sides], axis=1)
    found = found.reshape(9, 2, positions).astype(jnp.int32) - 1
    at = jnp.arange(9, dtype=jnp.int32)
    step = (jnp.stack([at // 3, at % 3], axis=1) - 1) * extent
    return jnp.where(found < 0, -extent, found + step[:, :, None])


def after(value, *others):
    return lax.optimization_barrier((value, *others))[0]


def chip_sum(both):
    return tree_sum([both[0]] + [flipped(both[t], "sy", 2 * t) for t in range(1, both.shape[0])])


def probe_fresh(parts, chunk):
    planes, rows, lanes = chunk.shape
    total = tree_sum(parts).reshape(planes + 1, rows, lanes)
    return chunk - PROBE_STEP * total[:planes] / (total[planes:] + REGULAR)


def across(total, start):
    return [total] + [flipped(total, "sx", t) for t in range(start, lax.axis_size("sx"))]


def probe_spread(fresh, chips):
    return jnp.stack([fresh] + [flipped(fresh, "sy", 2 * t) for t in range(1, chips)])


def per_device(object_tile, probe_modes, scan_offsets, intensities):
    tile = object_tile.shape[1]
    modes, _, extent, _ = probe_modes.shape
    halo = extent // 2
    size = tile + 2 * halo
    chips = lax.axis_size("sy") // 2
    rows = extent // 2 // chips
    planes = 2 * modes
    measured = intensities[0, 0]
    table = jnp.asarray(dft_tables(extent))
    scal = head_scalars(size, halo)
    offsets = scan_offsets[0, 0]
    positions = offsets.shape[0]
    offs = offsets.T
    kept = (chips, planes + 1, rows, extent)
    count = chips * (planes + 1) * rows
    rim_rows = 2 * 2 * halo
    quadrants = (f32(2, 2, tile, tile),) * 2
    rims = (f32(2, 2, tile, tile), f32(rim_rows, tile))
    scratch = ((2, 2, size, tile), (planes + 1, extent, extent))
    work = 2 * 3 * positions * 4 * (2 * extent) ** 3

    start = (lax.axis_index("sy") % 2 * chips + lax.axis_index("sy") // 2) * rows
    chunk = lax.dynamic_slice_in_dim(probe_modes.reshape(planes, extent, extent), start, rows, axis=1)
    halos = fetch(object_tile, offs, halo)

    def light(probe, corners):
        lit = (2, 2 * size, extent)
        return kernel_call(light_kernel, f32(2, size, tile), (scal, corners, probe), [lit], flops=work // 2)

    probe = probe_modes
    for iteration in range(ITERS):
        final = iteration == ITERS - 1
        sent = (count + rim_rows, extent) if final else kept
        outs = (rims if final else quadrants) + (f32(*kept), f32(*sent), f32(2, 2, size, tile))
        if iteration == 0:
            operands = (scal, offs, object_tile, *halos, probe, measured, table)
            outs = (f32(24, tile),) + outs
            reaches, *given, keep, send, canvas = kernel_call(first_kernel, outs, operands, scratch, flops=work)
        else:
            operands = (scal, offs, canvas, scale, near, far, own, other, measured, table)
            outs = outs + (f32(*probe.shape),)
            *given, keep, send, canvas, probe = kernel_call(next_kernel, outs, operands, scratch, flops=work)
        received = swapped(send, "sy", False)
        both = keep + received.reshape(-1, extent)[:count].reshape(kept)
        if iteration == 0:
            corners = corners_of(after(reaches, both), positions, tile)
        scale = light(probe, after(corners, both))
        if not final:
            side_b = given[1] + partnered(swapped(given[1], "sx", True), "sx")
            side_a = given[0] + swapped(given[0], "sx", False)
            near, far = jnp.stack([side_a[0], side_b[0]]), jnp.stack([side_a[1], side_b[1]])
            near = near + swapped(near, "sy", False)
            far = far + partnered(swapped(far, "sy", True), "sy")
            total = after(chip_sum(both), near, scale)
            chunk = after(probe_fresh(across(total, 1), chunk), near, far)
        else:
            own_rows, far = given
            far = swapped(far, "sy", True)
            total = after(chip_sum(both), far, scale)
            far = partnered(after(far, total), "sy")
            middle, near, far = kernel_call(
                middle_kernel, (f32(2, tile, tile),) + (f32(tile, tile),) * 2, (scal, own_rows, received, far), scalars=1
            )
            near = swapped(near, "sx", False)
            far = partnered(swapped(far, "sx", True), "sx")
            parts = across(total, 1)
            chunk = probe_fresh(parts, chunk)
            outcome = kernel_call(object_kernel, f32(2, tile, tile), (scal, canvas, scale, middle, near, far), scalars=1)
        own = probe_spread(chunk, chips)
        other = swapped(after(own, outcome) if final else own, "sy", False)
    return outcome, kernel_call(last_kernel, f32(*probe.shape), (scal, own, other), scalars=1)


def solution(mesh):
    placed = (P(None, "sy", "sx"), P(), P("sy", "sx", None, None), P("sy", "sx", None, None, None))
    return jax.shard_map(
        per_device,
        mesh=mesh,
        in_specs=placed,
        out_specs=(P(None, "sy", "sx"), P()),
        check_vma=False,
    )
```

```python
import functools

import jax
import jax.numpy as jnp
import numpy as np
from jax import lax
from jax.experimental import pallas as pl
from jax.experimental.pallas import tpu as pltpu
from jax.sharding import PartitionSpec as P

ITERS = 2
OBJECT_STEP = 0.5
PROBE_STEP = 2.0
REGULAR = 1.0


def dft_tables(extent):
    line = np.arange(extent)
    angle = (line[:, None] * line[None, :] % extent) * (2.0 * np.pi / extent)
    cosine, sine = np.cos(angle) / np.sqrt(extent), np.sin(angle) / np.sqrt(extent)
    table = np.block([[cosine, -sine], [sine, cosine]])
    high = table.astype(jnp.bfloat16)
    low = (table - high.astype(np.float64)).astype(jnp.bfloat16)
    return np.stack([high, low, high.T, low.T])


def split(values):
    high = values.astype(jnp.bfloat16)
    return high, (values - high.astype(jnp.float32)).astype(jnp.bfloat16)


def product(left, right):
    dot = functools.partial(jnp.dot, preferred_element_type=jnp.float32)
    return dot(left[0], right[0]) + (dot(left[0], right[1]) + dot(left[1], right[0]))


def swapped(values, axis, odd):
    if not odd:
        return lax.ppermute(values, axis, [(i, i ^ 1) for i in range(lax.axis_size(axis))])
    rows, cols = lax.axis_size("sy"), lax.axis_size("sx")
    pairs = []
    for row in range(rows):
        for col in range(cols):
            to_row, to_col = row, col
            if axis == "sy":
                if 0 < row < rows - 1:
                    to_row = row + 1 if row % 2 else row - 1
                else:
                    to_col = col ^ 1
            elif 0 < col < cols - 1:
                to_col = col + 1 if col % 2 else col - 1
            else:
                to_row = row ^ 1
            pairs.append((row * cols + col, to_row * cols + to_col))
    return lax.ppermute(values, ("sy", "sx"), pairs)


def partnered(received, axis):
    at = lax.axis_index(axis)
    return jnp.where((at == 0) | (at == lax.axis_size(axis) - 1), 0.0, received)


def flipped(values, axis, bits):
    return lax.ppermute(values, axis, [(i, i ^ bits) for i in range(lax.axis_size(axis))])


def tree_sum(parts):
    while len(parts) > 1:
        parts = [parts[i] + parts[i + 1] for i in range(0, len(parts), 2)]
    return parts[0]


def head_scalars(canvas_size, halo):
    row, col = lax.axis_index("sy"), lax.axis_index("sx")
    rows, cols = lax.axis_size("sy"), lax.axis_size("sx")
    head = [
        row % 2,
        col % 2,
        row // 2,
        jnp.where(row == 0, halo, 0),
        jnp.where(row == rows - 1, canvas_size - halo, canvas_size),
        jnp.where(col == 0, halo, 0),
        jnp.where(col == cols - 1, canvas_size - halo, canvas_size),
    ]
    return jnp.stack(head).astype(jnp.int32)


HEAD = 7


def light_kernel(scal, corners, probe_ref, scale_ref, lit):
    _, size, extent = scale_ref.shape
    lit[...] = jnp.zeros_like(lit)
    weight = sum(probe_ref[k, part] * probe_ref[k, part] for k in range(probe_ref.shape[0]) for part in range(2))
    lane = lax.broadcasted_iota(jnp.int32, (extent, extent), 1)

    for device in range(corners.shape[0]):
        for j in range(corners.shape[2]):
            row, col = corners[device, 0, j] + extent, corners[device, 1, j]
            moved = pltpu.roll(weight, col & (extent - 1), 1)
            for side in range(2):
                if device % 3 == 2 * (1 - side):
                    continue
                covered = (lane + side * extent >= col) & (lane + side * extent < col + extent)
                lit[side, pl.ds(row, extent), :] += jnp.where(covered, moved, 0.0)
    at_row = lax.broadcasted_iota(jnp.int32, (size, extent), 0)
    at_col = lax.broadcasted_iota(jnp.int32, (size, extent), 1)
    for side in range(2):
        inside = (at_row >= scal[3]) & (at_row < scal[4]) & (at_col + side * extent >= scal[5])
        inside = inside & (at_col + side * extent < scal[6])
        lighting = lit[side, extent : extent + size, :]
        scale_ref[side] = jnp.where(inside, OBJECT_STEP / (lighting + REGULAR), 0.0)


def updated_canvas(scal, old_ref, scale_ref, sums, canvas_ref):
    half = old_ref.shape[-1]
    for a in range(2):
        row = pl.multiple_of(jnp.where(scal[0] == a, half, 0), half)
        for b in range(2):
            side = jnp.where(scal[1] == b, 1, 0)
            scale = scale_ref[side, pl.ds(row, half)]
            for part in range(2):
                here = (part, side, pl.ds(row, half))
                canvas_ref[here] = old_ref[here] - scale * sums[a][b, part]


def place_probe(scal, own_ref, other_ref, probe_ref):
    chips, planes, rows, _ = own_ref.shape
    for slot in range(chips):
        chunk = scal[2] ^ slot
        for which, ref in ((scal[0], own_ref), (1 - scal[0], other_ref)):
            start = pl.multiple_of((which * chips + chunk) * rows, rows)
            for plane in range(planes):
                probe_ref[plane // 2, plane % 2, pl.ds(start, rows), :] = ref[slot, plane]


def terms_body(scal, offs, canvas_ref, probe_ref, measured_ref, table_ref, outs, keep_out, send_out, grad, sums):
    positions, extent, _ = measured_ref.shape
    modes = probe_ref.shape[0]
    w1 = (table_ref[0], table_ref[1])
    w2 = (table_ref[2], table_ref[3])
    grad[...] = jnp.zeros_like(grad)
    lane = lax.broadcasted_iota(jnp.int32, (extent, extent), 1)
    group = positions
    for first in range(0, positions, group):
        span = range(first, min(first + group, positions))
        patches = []
        for j in span:
            row, col = offs[0, j], offs[1, j]
            back = (extent - col) & (extent - 1)
            patches.append([
                jnp.where(
                    lane < extent - col,
                    pltpu.roll(canvas_ref[part, 0, pl.ds(row, extent), :], back, 1),
                    pltpu.roll(canvas_ref[part, 1, pl.ds(row, extent), :], back, 1),
                )
                for part in range(2)
            ])
        waves = []
        for o_r, o_i in patches:
            for k in range(modes):
                p_r, p_i = probe_ref[k, 0], probe_ref[k, 1]
                waves.append(jnp.concatenate([p_r * o_r - p_i * o_i, p_r * o_i + p_i * o_r], axis=1))
        count = len(waves)
        half = product(split(jnp.concatenate(waves, axis=0)), w1)
        rows = [half[k * extent : (k + 1) * extent] for k in range(count)]
        half = jnp.concatenate(
            [jnp.concatenate([r[:, part * extent : (part + 1) * extent] for r in rows], axis=1) for part in range(2)],
            axis=0,
        )
        spectrum = product(w2, split(half))
        squares = spectrum * spectrum
        power = squares[:extent] + squares[extent:]
        wide = []
        for at, j in enumerate(span):
            misfit = sum(power[:, k * extent : (k + 1) * extent] for k in range(at * modes, (at + 1) * modes)) - measured_ref[j]
            wide += [misfit] * modes
        wide = jnp.concatenate(wide, axis=1)
        weighted = spectrum * jnp.concatenate([wide, wide], axis=0)
        half = product(w1, split(weighted))
        half = jnp.concatenate(
            [
                jnp.concatenate([half[:extent, k * extent : (k + 1) * extent], half[extent:, k * extent : (k + 1) * extent]], axis=1)
                for k in range(count)
            ],
            axis=0,
        )
        chi = product(split(half), w2)
        for at, j in enumerate(span):
            o_r, o_i = patches[at]
            row, col = offs[0, j], offs[1, j]
            turn = col & (extent - 1)
            g_r = g_i = 0.0
            for k in range(modes):
                p_r, p_i = probe_ref[k, 0], probe_ref[k, 1]
                wave = at * modes + k
                c_r = chi[wave * extent : (wave + 1) * extent, :extent]
                c_i = chi[wave * extent : (wave + 1) * extent, extent:]
                g_r = g_r + (p_r * c_r + p_i * c_i)
                g_i = g_i + (p_r * c_i - p_i * c_r)
                for part, term in ((0, o_r * c_r + o_i * c_i), (1, o_r * c_i - o_i * c_r)):
                    plane = 2 * k + part
                    sums[plane] = term if j == 0 else sums[plane] + term
            term = o_r * o_r + o_i * o_i
            sums[2 * modes] = term if j == 0 else sums[2 * modes] + term
            for plane, term in enumerate((g_r, g_i)):
                moved = pltpu.roll(term, turn, 1)
                grad[plane, 0, pl.ds(row, extent), :] += jnp.where(lane >= col, moved, 0.0)
                grad[plane, 1, pl.ds(row, extent), :] += jnp.where(lane < col, moved, 0.0)
    if len(outs[0].shape) == len(outs[1].shape):
        give_quadrants(scal, grad, outs)
    else:
        give_rims(scal, grad, outs, send_out)
    chips, planes, rows, _ = keep_out.shape
    for slot in range(chips):
        chunk = scal[2] ^ slot
        for which, ref in ((scal[0], keep_out), (1 - scal[0], send_out)):
            start = pl.multiple_of((which * chips + chunk) * rows, rows)
            for plane in range(planes):
                piece = sums[plane, pl.ds(start, rows), :]
                if len(ref.shape) == 2:
                    at = (slot * planes + plane) * rows
                    ref[at : at + rows, :] = piece
                else:
                    ref[slot, plane] = piece


def give_quadrants(scal, grad, outs):
    extent = grad.shape[-1]
    for a in range(2):
        row = pl.multiple_of(jnp.where(scal[0] == a, extent, 0), extent)
        for b in range(2):
            side = jnp.where(scal[1] == b, 1, 0)
            for plane in range(grad.shape[0]):
                outs[b][a, plane] = grad[plane, side, pl.ds(row, extent), :]


def give_rims(scal, grad, outs, send_out):
    planes, sides, size, extent = grad.shape
    halo = extent // 2
    base = send_out.shape[0] - planes * sides * halo
    outer = (pl.multiple_of(jnp.where(scal[0] == 1, 0, size - halo), halo), pl.multiple_of(jnp.where(scal[0] == 1, size - halo, 0), halo))
    for plane in range(planes):
        for side in range(sides):
            at = (plane * sides + side) * halo
            outs[0][plane, side] = grad[plane, side, halo : size - halo, :]
            send_out[base + at : base + at + halo, :] = grad[plane, side, pl.ds(outer[0], halo), :]
            outs[1][at : at + halo, :] = grad[plane, side, pl.ds(outer[1], halo), :]


def middle_kernel(scal, own_ref, near_ref, far_ref, middle_ref, near_out, far_out):
    planes, sides, extent, _ = own_ref.shape
    halo = extent // 2
    base = near_ref.shape[0] - planes * sides * halo
    odd_row, odd_col = scal[0] == 1, scal[1] == 1
    lane = lax.broadcasted_iota(jnp.int32, (extent, extent), 1)
    rims = []
    for plane in range(planes):
        rows = []
        for side in range(sides):
            at = (plane * sides + side) * halo
            near, far = near_ref[base + at : base + at + halo, :], far_ref[at : at + halo, :]
            other = jnp.concatenate([jnp.where(odd_row, near, far), jnp.where(odd_row, far, near)], axis=0)
            rows.append(own_ref[plane, side] + other)
        turned = [pltpu.roll(part, halo, 1) for part in rows]
        middle_ref[plane] = jnp.where(lane < halo, turned[0], turned[1])
        rims.append((rows[0], turned[1]) if plane == 0 else (turned[0], rows[1]))
    left, right = (jnp.where(lane < halo, rims[0][side], rims[1][side]) for side in range(sides))
    near_out[...] = jnp.where(odd_col, left, right)
    far_out[...] = jnp.where(odd_col, right, left)


def object_kernel(scal, old_ref, scale_ref, middle_ref, near_ref, far_ref, object_ref):
    extent = old_ref.shape[-1]
    halo = extent // 2
    lane = lax.broadcasted_iota(jnp.int32, (extent, extent), 1)
    middle = pl.ds(halo, extent)

    def tile_of(sides):
        return jnp.where(lane < halo, pltpu.roll(sides[0], halo, 1), pltpu.roll(sides[1], halo, 1))

    scale = tile_of([scale_ref[side, middle] for side in range(2)])
    odd = scal[1] == 1
    near, far = near_ref[...], far_ref[...]
    left = jnp.where(scal[5] > 0, 0.0, jnp.where(odd, near, far))
    right = jnp.where(scal[6] < 2 * extent, 0.0, jnp.where(odd, far, near))
    for part in range(2):
        if part == 0:
            beside = jnp.where(lane < halo, left, pltpu.roll(right, halo, 1))
        else:
            beside = jnp.where(lane < halo, pltpu.roll(left, halo, 1), right)
        old = tile_of([old_ref[part, side, middle] for side in range(2)])
        object_ref[part] = old - scale * (middle_ref[part] + beside)


def first_kernel(
    scal, offs, tile_ref, rows_near, rows_far, cols_near, cols_far, reach, probe_ref, measured_ref, table_ref,
    reaches_out, *rest,
):
    reaches_out[0:8, :], reaches_out[8:16, :], reaches_out[16:24, :] = cols_near[-8:, :], cols_far[-8:, :], reach[...]
    outs, (keep_out, send_out, canvas_ref, grad, sums) = rest[:-5], rest[-5:]
    extent = tile_ref.shape[-1]
    halo = extent // 2
    size = 2 * extent
    odd_row, odd_col = scal[0] == 1, scal[1] == 1
    lane = lax.broadcasted_iota(jnp.int32, (extent, extent), 1)
    for part in range(2):
        near, far = (ref[part * halo : (part + 1) * halo] for ref in (rows_near, rows_far))
        above, below = jnp.where(odd_row, near, far), jnp.where(odd_row, far, near)
        for start in range(0, size, extent):
            half = pl.ds(start, extent)
            if start == 0:
                middle = jnp.concatenate([above, tile_ref[part, :halo]], axis=0)
            else:
                middle = jnp.concatenate([tile_ref[part, halo:], below], axis=0)
            middle = pltpu.roll(middle, halo, 1)
            near, far = cols_near[half], cols_far[half]
            if part == 1:
                near, far = pltpu.roll(near, halo, 1), pltpu.roll(far, halo, 1)
            left, right = jnp.where(odd_col, near, far), jnp.where(odd_col, far, near)
            canvas_ref[part, 0, half] = jnp.where(lane < halo, left, middle)
            canvas_ref[part, 1, half] = jnp.where(lane < halo, middle, pltpu.roll(right, halo, 1))
    terms_body(scal, offs, canvas_ref, probe_ref, measured_ref, table_ref, outs, keep_out, send_out, grad, sums)


def next_kernel(scal, offs, old_ref, scale_ref, near_ref, far_ref, own_ref, other_ref, measured_ref, table_ref, *rest):
    outs, (keep_out, send_out, canvas_ref, probe_ref, grad, sums) = rest[:-6], rest[-6:]
    updated_canvas(scal, old_ref, scale_ref, (near_ref, far_ref), canvas_ref)
    place_probe(scal, own_ref, other_ref, probe_ref)
    terms_body(scal, offs, canvas_ref, probe_ref, measured_ref, table_ref, outs, keep_out, send_out, grad, sums)


def last_kernel(scal, own_ref, other_ref, probe_ref):
    place_probe(scal, own_ref, other_ref, probe_ref)


SMEM = pl.BlockSpec(memory_space=pltpu.SMEM)
VMEM = pl.BlockSpec(memory_space=pltpu.VMEM)
PARAMS = pltpu.CompilerParams(vmem_limit_bytes=32 * 1024 * 1024)


def f32(*shape):
    return jax.ShapeDtypeStruct(shape, jnp.float32)


def kernel_call(body, outs, operands, scratch=(), scalars=2, flops=0):
    return pl.pallas_call(
        body,
        out_shape=outs,
        in_specs=[SMEM] * scalars + [VMEM] * (len(operands) - scalars),
        out_specs=jax.tree.map(lambda _: VMEM, outs),
        scratch_shapes=[pltpu.VMEM(shape, jnp.float32) for shape in scratch],
        compiler_params=PARAMS,
        cost_estimate=pl.CostEstimate(flops=flops, bytes_accessed=1 << 20, transcendentals=0),
    )(*operands)


def fetch(tile, offs, halo):
    lanes = tile.shape[-1]
    odd_row, odd_col = (lax.axis_index(axis) % 2 == 1 for axis in ("sy", "sx"))
    upper, lower = tile[:, :halo].reshape(-1, lanes), tile[:, halo:].reshape(-1, lanes)
    near, far = jnp.where(odd_row, upper, lower), jnp.where(odd_row, lower, upper)
    own = jnp.pad((after(offs, near, far) + 1).astype(jnp.float32), ((0, 6), (0, lanes - offs.shape[1])))
    near, far = jnp.concatenate([near, own]), jnp.concatenate([far, own])
    rows_near, rows_far = swapped(near, "sy", False), partnered(swapped(far, "sy", True), "sy")
    side = after(tile, near, far)
    left = jnp.concatenate([side[0, :, :halo], side[1, :, :halo]], axis=1)
    right = jnp.concatenate([side[0, :, halo:], side[1, :, halo:]], axis=1)
    left, right = jnp.where(odd_col, left, right), jnp.where(odd_col, right, left)
    above, below = jnp.where(odd_row, rows_near, rows_far), jnp.where(odd_row, rows_far, rows_near)
    last = 2 * halo
    reach = jnp.concatenate([above[last : last + 2], own[:2], below[last : last + 2], own[6:]])

    def columns_of(middle, first):
        ends = []
        for rim in (above, below):
            rim = rim[:last].reshape(2, halo, lanes)
            half = [jnp.where(first, rim[part, :, :halo], rim[part, :, halo:]) for part in range(2)]
            ends.append(jnp.concatenate(half, axis=1))
        return jnp.concatenate([ends[0], middle, ends[1], reach])

    cols_near = swapped(columns_of(left, odd_col), "sx", False)
    cols_far = partnered(swapped(columns_of(right, ~odd_col), "sx", True), "sx")
    return rows_near, rows_far, cols_near, cols_far, reach


def corners_of(reaches, positions, extent):
    near, far, own = reaches[:8], reaches[8:16], reaches[16:]
    odd = lax.axis_index("sx") % 2 == 1
    sides = [jnp.where(odd, near, far), own, jnp.where(odd, far, near)]
    found = jnp.stack([side[:6, :positions].reshape(3, 2, positions) for side in sides], axis=1)
    found = found.reshape(9, 2, positions).astype(jnp.int32) - 1
    at = jnp.arange(9, dtype=jnp.int32)
    step = (jnp.stack([at // 3, at % 3], axis=1) - 1) * extent
    return jnp.where(found < 0, -extent, found + step[:, :, None])


def after(value, *others):
    return lax.optimization_barrier((value, *others))[0]


def chip_sum(both):
    return tree_sum([both[0]] + [flipped(both[t], "sy", 2 * t) for t in range(1, both.shape[0])])


def probe_fresh(parts, chunk):
    planes, rows, lanes = chunk.shape
    total = tree_sum(parts).reshape(planes + 1, rows, lanes)
    return chunk - PROBE_STEP * total[:planes] / (total[planes:] + REGULAR)


def across(total, start):
    return [total] + [flipped(total, "sx", t) for t in range(start, lax.axis_size("sx"))]


def probe_spread(fresh, chips, *others):
    first = flipped(fresh, "sy", 2 * (chips - 1))
    sent = after(fresh, *others) if others else fresh
    return jnp.stack([fresh] + [flipped(sent, "sy", 2 * t) for t in range(1, chips - 1)] + [first])


def per_device(object_tile, probe_modes, scan_offsets, intensities):
    tile = object_tile.shape[1]
    modes, _, extent, _ = probe_modes.shape
    halo = extent // 2
    size = tile + 2 * halo
    chips = lax.axis_size("sy") // 2
    rows = extent // 2 // chips
    planes = 2 * modes
    measured = intensities[0, 0]
    table = jnp.asarray(dft_tables(extent))
    scal = head_scalars(size, halo)
    offsets = scan_offsets[0, 0]
    positions = offsets.shape[0]
    offs = offsets.T
    kept = (chips, planes + 1, rows, extent)
    count = chips * (planes + 1) * rows
    rim_rows = 2 * 2 * halo
    quadrants = (f32(2, 2, tile, tile),) * 2
    rims = (f32(2, 2, tile, tile), f32(rim_rows, tile))
    scratch = ((2, 2, size, tile), (planes + 1, extent, extent))
    work = 2 * 3 * positions * 4 * (2 * extent) ** 3

    start = (lax.axis_index("sy") % 2 * chips + lax.axis_index("sy") // 2) * rows
    chunk = lax.dynamic_slice_in_dim(probe_modes.reshape(planes, extent, extent), start, rows, axis=1)
    halos = fetch(object_tile, offs, halo)

    def light(probe, corners):
        lit = (2, 2 * size, extent)
        return kernel_call(light_kernel, f32(2, size, tile), (scal, corners, probe), [lit], flops=work // 2)

    probe = probe_modes
    for iteration in range(ITERS):
        final = iteration == ITERS - 1
        sent = (count + rim_rows, extent) if final else kept
        outs = (rims if final else quadrants) + (f32(*kept), f32(*sent), f32(2, 2, size, tile))
        if iteration == 0:
            operands = (scal, offs, object_tile, *halos, probe, measured, table)
            outs = (f32(24, tile),) + outs
            reaches, *given, keep, send, canvas = kernel_call(first_kernel, outs, operands, scratch, flops=work)
        else:
            operands = (scal, offs, canvas, scale, near, far, own, other, measured, table)
            outs = outs + (f32(*probe.shape),)
            *given, keep, send, canvas, probe = kernel_call(next_kernel, outs, operands, scratch, flops=work)
        received = swapped(send, "sy", False)
        both = keep + received.reshape(-1, extent)[:count].reshape(kept)
        if iteration == 0:
            corners = corners_of(after(reaches, both), positions, tile)
        scale = light(probe, after(corners, both))
        if not final:
            side_b = given[1] + partnered(swapped(given[1], "sx", True), "sx")
            side_a = given[0] + swapped(given[0], "sx", False)
            near, far = jnp.stack([side_a[0], side_b[0]]), jnp.stack([side_a[1], side_b[1]])
            near = near + swapped(near, "sy", False)
            far = far + partnered(swapped(far, "sy", True), "sy")
            total = after(chip_sum(both), near, scale)
            chunk = probe_fresh(across(total, 1), chunk)
        else:
            own_rows, far = given
            far = swapped(far, "sy", True)
            total = after(chip_sum(both), far, scale)
            far = partnered(after(far, total), "sy")
            middle, near, far = kernel_call(
                middle_kernel, (f32(2, tile, tile),) + (f32(tile, tile),) * 2, (scal, own_rows, received, far), scalars=1
            )
            near = swapped(near, "sx", False)
            far = partnered(swapped(far, "sx", True), "sx")
            parts = across(total, 1)
            chunk = probe_fresh(parts, chunk)
            outcome = kernel_call(object_kernel, f32(2, tile, tile), (scal, canvas, scale, middle, near, far), scalars=1)
        own = probe_spread(chunk, chips) if final else probe_spread(chunk, chips, near, far)
        other = swapped(after(own, outcome) if final else own, "sy", False)
    return outcome, kernel_call(last_kernel, f32(*probe.shape), (scal, own, other), scalars=1)


def solution(mesh):
    placed = (P(None, "sy", "sx"), P(), P("sy", "sx", None, None), P("sy", "sx", None, None, None))
    return jax.shard_map(
        per_device,
        mesh=mesh,
        in_specs=placed,
        out_specs=(P(None, "sy", "sx"), P()),
        check_vma=False,
    )
```
